256 devices in a mesh: ctx: 128 (over x, z, y), head: 2 (over core).
Axes of the slice: x: 4, y: 4, z: 8, core: 2. Of those that a mesh axis runs over, the one named last changes fastest.
Arguments:
- queries: bfloat16 [65536, 2048], P('ctx', 'head'), may hold values from -24 to 24
- keys: bfloat16 [65536, 2048], P('ctx', 'head'), may hold values from -24 to 24
- values: bfloat16 [65536, 2048], P('ctx', 'head'), may hold values from -6 to 6
- prefix_keys: bfloat16 [65536, 2048], P('ctx', 'head'), may hold values from -6 to 6
- prefix_values: bfloat16 [65536, 2048], P('ctx', 'head'), may hold values from -6 to 6
- selected: int32 [2, 512, 8, 3], P('head', 'ctx'), may hold values from 0 to 127, all different within a row; in each aligned block of 32 rows (0 to 31, 32 to 63, ..., all dimensions but the last counted through in order) no two rows name the same one
- out_weight: bfloat16 [2, 1024, 4096], P('head', 'ctx'), may hold values from -0.125 to 0.125
Outputs:
- mixed: bfloat16 [65536, 4096], P('ctx', 'head')
The draws below stay inside these ranges and needn't reach their ends.
Inputs may be any that keep to these rules, and one draw needn't show every extreme that they name: `selected`: for every head group, tile and head, 3 different prefix blocks. Among the 32 rows of one device (one head group, that device's tiles), no block is named more than 1 times.
All inputs are finite; a program needn't handle non-finite values.
Results may differ from the reference program's by a relative error of at most 0.0056.
Values may be sent and summed in bfloat16 or wider, within the bound.
A program may use at most 128 MiB of HBM per device.

```python
import math
import jax
import jax.numpy as jnp
import numpy as np
from jax import lax

D = 4096
HEADS = 16
D_HEAD = 128
TILE = 128
BLOCK = 512
TOPK = 3
HEADS_DEV = 8
GROUPS = 2
TILES_DEV = 4
NEW_TOKENS = 65536
PREFIX_TOKENS = 65536
TILES = 512
PREFIX_BLOCKS = 128
CAP = 1


def drawn_base(key, salt):
    drawn = jax.random.normal(jax.random.fold_in(key, salt), (NEW_TOKENS, HEADS * D_HEAD), jnp.float32)
    return jnp.clip(drawn, -6.0, 6.0)


def draw_queries(key, part):
    drawn = drawn_base(key, 1)
    return drawn.astype(jnp.bfloat16)


def draw_keys(key, part):
    drawn = drawn_base(key, 2)
    return drawn.astype(jnp.bfloat16)


def block_levels(stream_key, shape, cuts, smallest, high):
    loudness = 1.0
    for dim, blocks in cuts:
        heights = jax.random.uniform(jax.random.fold_in(jax.random.fold_in(stream_key, 6), dim), (blocks,), jnp.float32, smallest / len(cuts), high / len(cuts))
        loudness = loudness * jnp.repeat(jnp.exp(heights), shape[dim] // blocks).reshape((-1,) + (1,) * (len(shape) - 1 - dim))
    return loudness


def shared_out(key, own, number, rows, number_of, top, most, lean):
    sequence = jax.random.permutation(key, number_of)
    packed, common = load_shares(number_of, rows * top, most, lean, True), load_shares(number_of, rows * top, most, lean, False)
    places = jnp.arange(number_of)

    def named(sizes, turn):
        used = int((sizes > 0).sum())
        fixed = max(1, used // 4)
        moved = fixed + (places - fixed + turn * (used - fixed)) % max(1, number_of - fixed)
        return jnp.zeros((number_of,), jnp.int32).at[sequence[jnp.where(places < fixed, places, moved)]].set(jnp.asarray(sizes, jnp.int32))

    sizes = jnp.where(number % 4 == 0, named(packed, number // 4), named(common, number - number // 4 - 1))
    mixed = jax.random.permutation(jax.random.fold_in(own, 3), number_of)
    giver, sink = mixed[0:number_of // 2 * 2:2], mixed[1:number_of // 2 * 2:2]
    room = jnp.minimum(sizes[giver] - 1, most - sizes[sink]) // 2
    room = jnp.where((giver == sequence[0]) | (sink == sequence[0]) | (sizes[sink] == 0), 0, jnp.maximum(room, 0))
    moved = jax.random.randint(jax.random.fold_in(own, 4), (number_of // 2,), 0, 1 << 20) % (room + 1)
    sizes = sizes.at[giver].add(-moved).at[sink].add(moved)
    members = jnp.searchsorted(jnp.cumsum(sizes), jnp.arange(rows * top), side="right").astype(jnp.int32)
    table = members.reshape(top, rows).T
    table = table[jax.random.permutation(jax.random.fold_in(own, 1), rows)]
    turn = jax.random.randint(jax.random.fold_in(own, 2), (rows, 1), 0, top)
    return jnp.take_along_axis(table, (jnp.arange(top)[None, :] + turn) % top, axis=1)


def load_shares(amount, total, reach, lean, full):
    weights = [(1 << 20) // math.isqrt(grade ** lean) + 1 for grade in range(1, amount + 1)]
    largest = reach if full else min(reach, max(-(-total // amount), total * weights[0] // sum(weights)))
    least = 1 if total - largest >= amount - 1 else 0
    holding, surplus = [largest] + [least] * (amount - 1), total - largest - least * (amount - 1)
    while surplus > 0:
        free = [i for i in range(1, amount) if holding[i] < largest] or [i for i in range(1, amount) if holding[i] < reach]
        mass, budget = sum([weights[i] for i in free]), surplus
        for i in free:
            addition = min(reach - holding[i], max(1, budget * weights[i] // mass), surplus)
            holding[i] = holding[i] + addition
            surplus = surplus - addition
    return np.array(holding)


def bell_draw(own_key, extent, deviation, reach, pieces=(), kind=jnp.bfloat16):
    values = jax.random.normal(own_key, extent, jnp.float32) * deviation
    if len(pieces) > 0:
        values = block_levels(own_key, extent, pieces, -0.22, 0.18) * values
    return jnp.clip(values, min=-reach, max=reach).astype(kind)


def setup_inputs(seed: int = 0) -> dict:
    streams_of = jax.random.split(jax.random.key(seed), 8)
    queries = draw_queries(jax.random.fold_in(streams_of[7], 71), 0)
    keys = draw_keys(jax.random.fold_in(streams_of[7], 71), 0)
    values = bell_draw(streams_of[2], (NEW_TOKENS, HEADS * D_HEAD), 1.0, 6.0, ((0, 128), (1, 2)))
    prefix_keys = bell_draw(streams_of[3], (PREFIX_TOKENS, HEADS * D_HEAD), 1.0, 6.0, ((0, 128), (1, 2)))
    prefix_values = bell_draw(streams_of[4], (PREFIX_TOKENS, HEADS * D_HEAD), 1.0, 6.0, ((0, 128), (1, 2)))
    selected_keys = jax.random.split(jax.random.fold_in(streams_of[5], 1), GROUPS * TILES * HEADS_DEV // (TILES_DEV * HEADS_DEV))
    selected_turns = jax.random.permutation(jax.random.fold_in(streams_of[5], 3), GROUPS * TILES * HEADS_DEV // (TILES_DEV * HEADS_DEV))
    selected = jax.vmap(lambda own, number: shared_out(jax.random.fold_in(streams_of[5], 2), own, number, TILES_DEV * HEADS_DEV, PREFIX_BLOCKS, TOPK, CAP, 2))(selected_keys, selected_turns).reshape((GROUPS, TILES, HEADS_DEV, TOPK))
    out_weight = bell_draw(streams_of[6], (GROUPS, HEADS_DEV * D_HEAD, D), (HEADS * D_HEAD) ** -0.5, 0.125, ((0, 2), (1, 128)))
    return dict(queries=queries, keys=keys, values=values, prefix_keys=prefix_keys, prefix_values=prefix_values, selected=selected, out_weight=out_weight)


def rounded(weights):
    narrow = weights.astype(jnp.bfloat16)
    narrow = lax.optimization_barrier(narrow)
    return narrow.astype(jnp.float32)


def reference(queries, keys, values, prefix_keys, prefix_values, selected, out_weight):
    score_scale = D_HEAD ** -0.5
    query_heads = queries.reshape(NEW_TOKENS, HEADS, D_HEAD)
    key_heads = keys.reshape(NEW_TOKENS, HEADS, D_HEAD)
    value_heads = values.reshape(NEW_TOKENS, HEADS, D_HEAD)
    prefix_key_table = prefix_keys.reshape(PREFIX_BLOCKS, BLOCK, HEADS, D_HEAD).transpose(0, 2, 1, 3)
    prefix_value_table = prefix_values.reshape(PREFIX_BLOCKS, BLOCK, HEADS, D_HEAD).transpose(0, 2, 1, 3)
    picked = selected.transpose(1, 0, 2, 3).reshape(TILES, HEADS, TOPK)
    head_ids = jnp.arange(HEADS, dtype=jnp.int32)

    def one_tile(tile_index):
        row_start = (tile_index * TILE).astype(jnp.int32)
        block_start = ((row_start // BLOCK) * BLOCK).astype(jnp.int32)
        query_tile = lax.dynamic_slice_in_dim(query_heads, row_start, TILE, 0).astype(jnp.float32)
        own_keys = lax.dynamic_slice_in_dim(key_heads, block_start, BLOCK, 0).astype(jnp.float32)
        own_values = lax.dynamic_slice_in_dim(value_heads, block_start, BLOCK, 0).astype(jnp.float32)
        scores = jnp.einsum("qhd,khd->hqk", query_tile, own_keys) * score_scale
        query_pos = row_start + jnp.arange(TILE, dtype=jnp.int32)
        key_pos = block_start + jnp.arange(BLOCK, dtype=jnp.int32)
        visible = key_pos[None, :] <= query_pos[:, None]
        scores = jnp.where(visible[None, :, :], scores, -jnp.inf)
        own_max = jnp.max(scores, axis=2)
        own_weights = jnp.exp(scores - own_max[:, :, None])
        own_sum = jnp.sum(own_weights, axis=2)
        own_out = jnp.einsum("hqk,khd->hqd", rounded(own_weights), own_values)
        tile_picks = picked[tile_index]
        sel_keys = prefix_key_table[tile_picks, head_ids[:, None]].astype(jnp.float32)
        sel_values = prefix_value_table[tile_picks, head_ids[:, None]].astype(jnp.float32)
        sel_scores = jnp.einsum("qhd,hjkd->hjqk", query_tile, sel_keys) * score_scale
        sel_max = jnp.max(sel_scores, axis=3)
        sel_weights = jnp.exp(sel_scores - sel_max[:, :, :, None])
        sel_sum = jnp.sum(sel_weights, axis=3)
        sel_out = jnp.einsum("hjqk,hjkd->hjqd", rounded(sel_weights), sel_values)
        highest = jnp.maximum(own_max, jnp.max(sel_max, axis=1))
        own_factor = jnp.exp(own_max - highest)
        sel_factor = jnp.exp(sel_max - highest[:, None, :])
        numerator = own_factor[:, :, None] * own_out + jnp.sum(sel_factor[:, :, :, None] * sel_out, axis=1)
        denominator = own_factor * own_sum + jnp.sum(sel_factor * sel_sum, axis=1)
        result = numerator / denominator[:, :, None]
        return result.transpose(1, 0, 2).reshape(TILE, HEADS * D_HEAD).astype(jnp.bfloat16)

    attention = lax.map(one_tile, jnp.arange(TILES, dtype=jnp.int32)).reshape(NEW_TOKENS, HEADS * D_HEAD)
    full_weight = out_weight.reshape(HEADS * D_HEAD, D)
    return jnp.dot(attention, full_weight, preferred_element_type=jnp.float32).astype(jnp.bfloat16)
```

```python
import functools
import math

import jax
import jax.numpy as jnp
from jax import lax
from jax.experimental import pallas as pl
from jax.experimental.pallas import tpu as pltpu
from jax.sharding import PartitionSpec as P

D_HEAD = 128
TILE = 128
BLOCK = 512
TOPK = 3
TILES = 4
HEADS = 8
ITEMS = TILES * HEADS
NX, NZ, NY = 4, 8, 4
PEERS = NX * NZ * NY
SCALE2 = D_HEAD**-0.5 * math.log2(math.e)


def coords(index):
    return index // (NZ * NY), (index // NY) % NZ, index % NY


def place(x, z, y):
    return (x * NZ + z) * NY + y


def offset_of(step):
    dz = (step * 3) % NZ
    dy = (step // NZ) % NY
    dx = (step // (NZ * NY)) % NX
    return dx, dz, dy


def moved(me, step, sign):
    x, z, y = coords(me)
    dx, dz, dy = offset_of(step)
    return place((x + sign * dx + NX) % NX, (z + sign * dz + NZ) % NZ, (y + sign * dy + NY) % NY)


def attend(key_block, value_block_t, query, mask=None):
    scores = lax.dot_general(
        key_block, query, (((1,), (1,)), ((), ())), preferred_element_type=jnp.float32
    )
    scores = scores * SCALE2
    if mask is not None:
        scores = jnp.where(mask, scores, -jnp.inf)
    top = jnp.max(scores, axis=0, keepdims=True)
    weights = jnp.exp2(scores - top)
    total = jnp.sum(weights, axis=0, keepdims=True)
    out = lax.dot_general(
        value_block_t,
        weights.astype(jnp.bfloat16),
        (((1,), (0,)), ((), ())),
        preferred_element_type=jnp.float32,
    )
    return out / total, top + jnp.log2(total)


def layer_kernel(
    wanted_ref,
    picked_ref,
    wanted_row_ref,
    q_ref,
    k_ref,
    v_ref,
    pk_ref,
    pv_ref,
    out_ref,
    items,
    send_q,
    recv_q,
    send_o,
    recv_o,
    send_l,
    recv_l,
    vt,
    own_o,
    own_l,
    table,
    table_s,
    table_sem,
    q_send_sem,
    q_recv_sem,
    o_send_sem,
    o_recv_sem,
    l_send_sem,
    l_recv_sem,
    t_send_sem,
    t_recv_sem,
    h_send_sem,
    h_recv_sem,
):
    me = lax.axis_index("ctx")
    core = lax.axis_index("head")
    x, z, y = coords(me)
    sign = 1 - 2 * core

    barrier = pltpu.get_barrier_semaphore()

    def greet(step, carry):
        pl.semaphore_signal(
            barrier,
            inc=1,
            device_id={"ctx": moved(me, step, 1)},
            device_id_type=pl.DeviceIdType.MESH,
        )
        return carry

    lax.fori_loop(1, PEERS, greet, 0)
    pl.semaphore_signal(
        barrier, inc=1, device_id={"head": 1 - core}, device_id_type=pl.DeviceIdType.MESH
    )

    for t in range(TILES):
        for h in range(HEADS):
            items[t * HEADS + h] = q_ref[
                t * TILE : (t + 1) * TILE, h * D_HEAD : (h + 1) * D_HEAD
            ]
    table[me] = wanted_row_ref[...]
    pl.semaphore_wait(barrier, PEERS)

    def table_copy(slot, rows, start, target):
        return pltpu.make_async_remote_copy(
            src_ref=table.at[pl.ds(start, rows)],
            dst_ref=table.at[pl.ds(start, rows)],
            send_sem=t_send_sem.at[slot],
            recv_sem=t_recv_sem.at[slot],
            device_id={"ctx": target},
            device_id_type=pl.DeviceIdType.MESH,
        )

    y_copies = [table_copy(d - 1, 1, me, place(x, z, (y + d) % NY)) for d in range(1, NY)]
    for c in y_copies:
        c.start()

    def q_copy(target, slot):
        return pltpu.make_async_remote_copy(
            src_ref=send_q.at[target],
            dst_ref=recv_q.at[slot],
            send_sem=q_send_sem.at[target],
            recv_sem=q_recv_sem.at[slot],
            device_id={"ctx": target},
            device_id_type=pl.DeviceIdType.MESH,
        )

    def send_query(step, carry):
        target = moved(me, step, sign)
        send_q[target] = items[wanted_ref[target]]
        q_copy(target, me).start()
        return carry

    lax.fori_loop(1, 17, send_query, 0)
    for d in range(1, NY):
        table_copy(d - 1, 1, place(x, z, (y - d + NY) % NY), me).wait_recv()
    z_copies = [
        table_copy(2 + d, NY, place(x, z, 0), place(x, (z + d) % NZ, y)) for d in range(1, NZ)
    ]
    for c in z_copies:
        c.start()
    lax.fori_loop(17, 49, send_query, 0)
    for d in range(1, NZ):
        table_copy(2 + d, NY, place(x, (z - d + NZ) % NZ, 0), me).wait_recv()
    x_copies = [
        table_copy(9 + d, NZ * NY, place(x, 0, 0), place((x + d) % NX, z, y))
        for d in range(1, NX)
    ]
    for c in x_copies:
        c.start()
    lax.fori_loop(49, PEERS, send_query, 0)

    for t in range(TILES):
        depth = (t + 1) * TILE
        row = lax.broadcasted_iota(jnp.int32, (depth, TILE), 0)
        column = lax.broadcasted_iota(jnp.int32, (depth, TILE), 1)
        mask = row <= column + t * TILE
        for h in range(HEADS):
            columns = slice(h * D_HEAD, (h + 1) * D_HEAD)
            out, lse = attend(
                k_ref[:depth, columns],
                v_ref[:depth, columns].T,
                q_ref[t * TILE : (t + 1) * TILE, columns],
                mask,
            )
            own_o[t * HEADS + h] = out
            own_l[t * HEADS + h] = lse
    for h in range(HEADS):
        columns = slice(h * D_HEAD, (h + 1) * D_HEAD)
        vt[h] = pv_ref[:, columns].T

    for d in range(1, NX):
        table_copy(9 + d, NZ * NY, place((x - d + NX) % NX, 0, 0), me).wait_recv()
    to_scalars = pltpu.make_async_copy(table, table_s, table_sem)
    to_scalars.start()
    to_scalars.wait()

    def o_copy(target, slot):
        return pltpu.make_async_remote_copy(
            src_ref=send_o.at[target],
            dst_ref=recv_o.at[slot],
            send_sem=o_send_sem.at[target],
            recv_sem=o_recv_sem.at[slot],
            device_id={"ctx": target},
            device_id_type=pl.DeviceIdType.MESH,
        )

    def l_copy(target, slot):
        return pltpu.make_async_remote_copy(
            src_ref=send_l.at[target],
            dst_ref=recv_l.at[slot],
            send_sem=l_send_sem.at[target],
            recv_sem=l_recv_sem.at[slot],
            device_id={"ctx": target},
            device_id_type=pl.DeviceIdType.MESH,
        )

    def answer(source, query):
        head = table_s[source, 0, me] % HEADS
        return attend(pk_ref[head], vt[head], query)

    out, lse = answer(me, items[wanted_ref[me]])
    recv_o[me] = out.astype(jnp.bfloat16)
    recv_l[me] = lse

    def serve(step, carry):
        source = moved(me, step, -sign)
        q_copy(me, source).wait_recv()
        out, lse = answer(source, recv_q[source])
        send_o[source] = out.astype(jnp.bfloat16)
        send_l[source] = lse
        o_copy(source, me).start()
        l_copy(source, me).start()
        return carry

    lax.fori_loop(1, PEERS, serve, 0)

    def settle(step, carry):
        server = moved(me, step, sign)
        o_copy(me, server).wait_recv()
        l_copy(me, server).wait_recv()
        return carry

    lax.fori_loop(1, PEERS, settle, 0)

    def h_copy(t):
        return pltpu.make_async_remote_copy(
            src_ref=out_ref.at[core, pl.ds(t * TILE, TILE)],
            dst_ref=out_ref.at[core, pl.ds(t * TILE, TILE)],
            send_sem=h_send_sem.at[t],
            recv_sem=h_recv_sem.at[t],
            device_id={"head": 1 - core},
            device_id_type=pl.DeviceIdType.MESH,
        )

    for t in range(TILES):
        for h in range(HEADS):
            item = t * HEADS + h
            slots = [picked_ref[item * TOPK + j] for j in range(TOPK)]
            lses = [own_l[item]] + [recv_l[s] for s in slots]
            highest = functools.reduce(jnp.maximum, lses)
            factors = [jnp.exp2(v - highest) for v in lses]
            total = functools.reduce(jnp.add, factors)
            mixed = factors[0] * own_o[item]
            for f, s in zip(factors[1:], slots):
                mixed = mixed + f * recv_o[s].astype(jnp.float32)
            mixed = mixed / total
            out_ref[core, t * TILE : (t + 1) * TILE, h * D_HEAD : (h + 1) * D_HEAD] = (
                mixed.T.astype(jnp.bfloat16)
            )
        h_copy(t).start()
    for t in range(TILES):
        pltpu.make_async_remote_copy(
            src_ref=out_ref.at[1 - core, pl.ds(t * TILE, TILE)],
            dst_ref=out_ref.at[1 - core, pl.ds(t * TILE, TILE)],
            send_sem=h_send_sem.at[t],
            recv_sem=h_recv_sem.at[t],
            device_id={"head": 1 - core},
            device_id_type=pl.DeviceIdType.MESH,
        ).wait_recv()
    for t in range(TILES):
        h_copy(t).wait_send()

    def drain(step, carry):
        target = moved(me, step, sign)
        q_copy(target, me).wait_send()
        source = moved(me, step, -sign)
        o_copy(source, me).wait_send()
        l_copy(source, me).wait_send()
        return carry

    lax.fori_loop(1, PEERS, drain, 0)
    for c in y_copies + z_copies + x_copies:
        c.wait_send()


def attention_layer(wanted, picked, queries, keys, values, prefix_keys, prefix_values):
    vmem = pl.BlockSpec(memory_space=pltpu.VMEM)
    smem = pl.BlockSpec(memory_space=pltpu.SMEM)
    slots = (PEERS, TILE, D_HEAD)
    sem = pltpu.SemaphoreType.DMA
    return pl.pallas_call(
        layer_kernel,
        out_shape=jax.ShapeDtypeStruct((2, BLOCK, HEADS * D_HEAD), jnp.bfloat16),
        in_specs=[smem, smem, vmem, vmem, vmem, vmem, vmem, vmem],
        out_specs=vmem,
        scratch_shapes=[
            pltpu.VMEM((ITEMS, TILE, D_HEAD), jnp.bfloat16),
            pltpu.VMEM(slots, jnp.bfloat16),
            pltpu.VMEM(slots, jnp.bfloat16),
            pltpu.VMEM(slots, jnp.bfloat16),
            pltpu.VMEM(slots, jnp.bfloat16),
            pltpu.VMEM((PEERS, 1, TILE), jnp.float32),
            pltpu.VMEM((PEERS, 1, TILE), jnp.float32),
            pltpu.VMEM((HEADS, D_HEAD, BLOCK), jnp.bfloat16),
            pltpu.VMEM((ITEMS, D_HEAD, TILE), jnp.float32),
            pltpu.VMEM((ITEMS, 1, TILE), jnp.float32),
            pltpu.VMEM((PEERS, 1, PEERS), jnp.int32),
            pltpu.SMEM((PEERS, 1, PEERS), jnp.int32),
            sem,
            sem((PEERS,)),
            sem((PEERS,)),
            sem((PEERS,)),
            sem((PEERS,)),
            sem((PEERS,)),
            sem((PEERS,)),
            sem((13,)),
            sem((13,)),
            sem((TILES,)),
            sem((TILES,)),
        ],
        compiler_params=pltpu.CompilerParams(
            collective_id=0, has_side_effects=True, vmem_limit_bytes=48 * 1024 * 1024
        ),
        cost_estimate=pl.CostEstimate(
            flops=6_000_000_000, bytes_accessed=700_000_000, transcendentals=10_000_000
        ),
    )(wanted, picked, wanted[None], queries, keys, values, prefix_keys, prefix_values)


def shards(queries, keys, values, prefix_keys, prefix_values, selected, out_weight):
    picked = selected.reshape(ITEMS * TOPK)
    matches = picked[None, :] == jnp.arange(PEERS, dtype=jnp.int32)[:, None]
    item_ids = jnp.arange(ITEMS * TOPK, dtype=jnp.int32) // TOPK
    wanted = jnp.sum(jnp.where(matches, item_ids[None, :], 0), axis=1)
    features = out_weight.shape[2] // 2
    swapped = lax.all_to_all(
        out_weight[0].reshape(-1, 2, features), "head", split_axis=1, concat_axis=1, tiled=True
    )
    weight = lax.all_gather(swapped.transpose(1, 0, 2), "ctx", axis=1, tiled=True)
    head_keys = prefix_keys.reshape(BLOCK, HEADS, D_HEAD).transpose(1, 0, 2)
    attention = attention_layer(
        wanted, picked, queries, keys, values, head_keys, prefix_values
    )
    return jnp.einsum(
        "gtr,grf->tf", attention, weight, preferred_element_type=jnp.float32
    ).astype(jnp.bfloat16)


def solution(mesh):
    return jax.shard_map(
        shards,
        mesh=mesh,
        in_specs=(
            P("ctx", "head"),
            P("ctx", "head"),
            P("ctx", "head"),
            P("ctx", "head"),
            P("ctx", "head"),
            P("head", "ctx", None, None),
            P("head", "ctx", None),
        ),
        out_specs=P("ctx", "head"),
        check_vma=False,
    )
```

```python
import functools
import math

import jax
import jax.numpy as jnp
from jax import lax
from jax.experimental import pallas as pl
from jax.experimental.pallas import tpu as pltpu
from jax.sharding import PartitionSpec as P

D_HEAD = 128
TILE = 128
BLOCK = 512
TOPK = 3
TILES = 4
HEADS = 8
ITEMS = TILES * HEADS
W_HALF = 1024
CHUNK = 512
NX, NZ, NY = 4, 8, 4
PEERS = NX * NZ * NY
SCALE2 = D_HEAD**-0.5 * math.log2(math.e)


def coords(index):
    return index // (NZ * NY), (index // NY) % NZ, index % NY


def place(x, z, y):
    return (x * NZ + z) * NY + y


def offset_of(step):
    dz = (step * 3) % NZ
    dy = (step // NZ) % NY
    dx = (step // (NZ * NY)) % NX
    return dx, dz, dy


def moved(me, step, sign):
    x, z, y = coords(me)
    dx, dz, dy = offset_of(step)
    return place((x + sign * dx + NX) % NX, (z + sign * dz + NZ) % NZ, (y + sign * dy + NY) % NY)


def attend(key_block, value_block_t, query, mask=None):
    scores = lax.dot_general(
        key_block, query, (((1,), (1,)), ((), ())), preferred_element_type=jnp.float32
    )
    scores = scores * SCALE2
    if mask is not None:
        scores = jnp.where(mask, scores, -jnp.inf)
    top = jnp.max(scores, axis=0, keepdims=True)
    weights = jnp.exp2(scores - top)
    total = jnp.sum(weights, axis=0, keepdims=True)
    out = lax.dot_general(
        value_block_t,
        weights.astype(jnp.bfloat16),
        (((1,), (0,)), ((), ())),
        preferred_element_type=jnp.float32,
    )
    return out / total, top + jnp.log2(total)


def layer_kernel(
    wanted_ref,
    picked_ref,
    wanted_row_ref,
    q_ref,
    k_ref,
    v_ref,
    pk_ref,
    pv_ref,
    w_ref,
    out_ref,
    items,
    send_q,
    recv_q,
    recv_o,
    send_l,
    recv_l,
    kh,
    vt,
    wbuf,
    wmat,
    att,
    acc,
    own_o,
    own_l,
    table,
    table_s,
    table_sem,
    q_send_sem,
    q_recv_sem,
    o_send_sem,
    o_recv_sem,
    l_send_sem,
    l_recv_sem,
    t_send_sem,
    t_recv_sem,
    h_send_sem,
    h_recv_sem,
    s_send_sem,
    s_recv_sem,
    w_send_sem,
    w_recv_sem,
):
    me = lax.axis_index("ctx")
    core = lax.axis_index("head")
    x, z, y = coords(me)
    sign = 1 - 2 * core

    barrier = pltpu.get_barrier_semaphore()

    def greet(step, carry):
        pl.semaphore_signal(
            barrier,
            inc=1,
            device_id={"ctx": moved(me, step, 1)},
            device_id_type=pl.DeviceIdType.MESH,
        )
        return carry

    lax.fori_loop(1, PEERS, greet, 0)
    pl.semaphore_signal(
        barrier, inc=1, device_id={"head": 1 - core}, device_id_type=pl.DeviceIdType.MESH
    )

    for t in range(TILES):
        for h in range(HEADS):
            items[t * HEADS + h] = q_ref[
                t * TILE : (t + 1) * TILE, h * D_HEAD : (h + 1) * D_HEAD
            ]
    table[me] = wanted_row_ref[...]
    pl.semaphore_wait(barrier, PEERS)

    def table_copy(slot, rows, start, target):
        return pltpu.make_async_remote_copy(
            src_ref=table.at[pl.ds(start, rows)],
            dst_ref=table.at[pl.ds(start, rows)],
            send_sem=t_send_sem.at[slot],
            recv_sem=t_recv_sem.at[slot],
            device_id={"ctx": target},
            device_id_type=pl.DeviceIdType.MESH,
        )

    def w_major(p):
        return x if p == 0 else y

    def w_minor(p):
        return y if p == 0 else x

    def w_device(p, major, minor, depth):
        return place(major, depth, minor) if p == 0 else place(minor, depth, major)

    def w_pos(p):
        return (w_major(p) * NY + w_minor(p)) * NZ + z

    def w_copy(p, slot, start, blocks, target):
        return pltpu.make_async_remote_copy(
            src_ref=wbuf.at[p, pl.ds(start, blocks)],
            dst_ref=wbuf.at[p, pl.ds(start, blocks)],
            send_sem=w_send_sem.at[p, slot],
            recv_sem=w_recv_sem.at[p, slot],
            device_id={"ctx": target},
            device_id_type=pl.DeviceIdType.MESH,
        )

    def s_copy(p):
        columns = pl.multiple_of((1 - core) * 2 * W_HALF + p * W_HALF, W_HALF)
        return pltpu.make_async_remote_copy(
            src_ref=w_ref.at[:, pl.ds(columns, W_HALF)],
            dst_ref=wbuf.at[p, w_pos(p), core],
            send_sem=s_send_sem.at[p],
            recv_sem=s_recv_sem.at[p],
            device_id={"head": 1 - core},
            device_id_type=pl.DeviceIdType.MESH,
        )

    w_started = []

    def w_send(p, slot, start, blocks, target):
        c = w_copy(p, slot, start, blocks, target)
        c.start()
        w_started.append(c)

    def w_line(p, level, ahead):
        if level == 0:
            minor = (w_minor(p) + ahead + 4) % 4
            return (w_major(p) * 4 + minor) * NZ, w_device(p, w_major(p), minor, z)
        major = (w_major(p) + ahead + 4) % 4
        return major * 4 * NZ, w_device(p, major, w_minor(p), z)

    def w_first(level):
        blocks = (NZ, 4 * NZ)[level]
        for p in range(2):
            start = w_line(p, level, 0)[0]
            w_send(p, 7 + 4 * level, start, blocks, w_line(p, level, 1)[1])
            w_send(p, 8 + 4 * level, start, blocks, w_line(p, level, -1)[1])

    def w_forward(level):
        blocks = (NZ, 4 * NZ)[level]
        half = blocks // 2
        for p in range(2):
            behind, ahead = w_line(p, level, -1), w_line(p, level, 1)
            w_copy(p, 7 + 4 * level, behind[0], blocks, me).wait_recv()
            w_send(p, 9 + 4 * level, behind[0], half, ahead[1])
            w_copy(p, 8 + 4 * level, ahead[0], blocks, me).wait_recv()
            w_send(p, 10 + 4 * level, ahead[0] + half, half, behind[1])

    def w_settle(level):
        half = (NZ, 4 * NZ)[level] // 2
        for p in range(2):
            opposite = w_line(p, level, 2)[0]
            w_copy(p, 9 + 4 * level, opposite, half, me).wait_recv()
            w_copy(p, 10 + 4 * level, opposite + half, half, me).wait_recv()

    for p in range(2):
        s_copy(p).start()
        columns = pl.multiple_of(core * 2 * W_HALF + p * W_HALF, W_HALF)
        wbuf[p, w_pos(p), core] = w_ref[:, pl.ds(columns, W_HALF)]

    y_copies = [table_copy(d - 1, 1, me, place(x, z, (y + d) % NY)) for d in range(1, NY)]
    for c in y_copies:
        c.start()

    for p in range(2):
        pltpu.make_async_remote_copy(
            src_ref=w_ref.at[:, pl.ds(0, W_HALF)],
            dst_ref=wbuf.at[p, w_pos(p), 1 - core],
            send_sem=s_send_sem.at[p],
            recv_sem=s_recv_sem.at[p],
            device_id={"head": 1 - core},
            device_id_type=pl.DeviceIdType.MESH,
        ).wait_recv()
        for d in range(1, NZ):
            w_send(
                p,
                d - 1,
                w_pos(p),
                1,
                w_device(p, w_major(p), w_minor(p), (z + d) % NZ),
            )

    def q_copy(target, slot):
        return pltpu.make_async_remote_copy(
            src_ref=send_q.at[target],
            dst_ref=recv_q.at[slot],
            send_sem=q_send_sem.at[target],
            recv_sem=q_recv_sem.at[slot],
            device_id={"ctx": target},
            device_id_type=pl.DeviceIdType.MESH,
        )

    def send_query(step, carry):
        target = moved(me, step, sign)
        send_q[target] = items[wanted_ref[target]]
        q_copy(target, me).start()
        return carry

    lax.fori_loop(1, 17, send_query, 0)
    for d in range(1, NY):
        table_copy(d - 1, 1, place(x, z, (y - d + NY) % NY), me).wait_recv()
    z_copies = [
        table_copy(2 + d, NY, place(x, z, 0), place(x, (z + d) % NZ, y)) for d in range(1, NZ)
    ]
    for c in z_copies:
        c.start()
    lax.fori_loop(17, 49, send_query, 0)
    for p in range(2):
        base = w_pos(p) - z
        for d in range(1, NZ):
            w_copy(p, d - 1, base + (z - d + NZ) % NZ, 1, me).wait_recv()
    w_first(0)
    for d in range(1, NZ):
        table_copy(2 + d, NY, place(x, (z - d + NZ) % NZ, 0), me).wait_recv()
    x_copies = [
        table_copy(9 + d, NZ * NY, place(x, 0, 0), place((x + d) % NX, z, y))
        for d in range(1, NX)
    ]
    for c in x_copies:
        c.start()
    lax.fori_loop(49, PEERS, send_query, 0)
    w_forward(0)

    for t in range(TILES):
        depth = (t + 1) * TILE
        row = lax.broadcasted_iota(jnp.int32, (depth, TILE), 0)
        column = lax.broadcasted_iota(jnp.int32, (depth, TILE), 1)
        mask = row <= column + t * TILE
        for h in range(HEADS):
            columns = slice(h * D_HEAD, (h + 1) * D_HEAD)
            out, lse = attend(
                k_ref[:depth, columns],
                v_ref[:depth, columns].T,
                q_ref[t * TILE : (t + 1) * TILE, columns],
                mask,
            )
            own_o[t * HEADS + h] = out
            own_l[t * HEADS + h] = lse
    for h in range(HEADS):
        columns = slice(h * D_HEAD, (h + 1) * D_HEAD)
        vt[h] = pv_ref[:, columns].T
        kh[h] = pk_ref[:, columns]
    w_settle(0)
    w_first(1)

    for d in range(1, NX):
        table_copy(9 + d, NZ * NY, place((x - d + NX) % NX, 0, 0), me).wait_recv()
    to_scalars = pltpu.make_async_copy(table, table_s, table_sem)
    to_scalars.start()
    to_scalars.wait()

    def o_copy(target, slot):
        return pltpu.make_async_remote_copy(
            src_ref=recv_q.at[target],
            dst_ref=recv_o.at[slot],
            send_sem=o_send_sem.at[target],
            recv_sem=o_recv_sem.at[slot],
            device_id={"ctx": target},
            device_id_type=pl.DeviceIdType.MESH,
        )

    def l_copy(target, slot):
        return pltpu.make_async_remote_copy(
            src_ref=send_l.at[target],
            dst_ref=recv_l.at[slot],
            send_sem=l_send_sem.at[target],
            recv_sem=l_recv_sem.at[slot],
            device_id={"ctx": target},
            device_id_type=pl.DeviceIdType.MESH,
        )

    def answer(source, query):
        head = table_s[source, 0, me] % HEADS
        return attend(kh[head], vt[head], query)

    out, lse = answer(me, items[wanted_ref[me]])
    recv_o[me] = out.astype(jnp.bfloat16)
    recv_l[me] = lse

    def serve(step, carry):
        source = moved(me, step, -sign)
        q_copy(me, source).wait_recv()
        out, lse = answer(source, recv_q[source])
        recv_q[source] = out.astype(jnp.bfloat16)
        send_l[source] = lse
        o_copy(source, me).start()
        l_copy(source, me).start()
        return carry

    lax.fori_loop(1, 56, serve, 0)
    w_forward(1)
    lax.fori_loop(56, PEERS, serve, 0)

    w_settle(1)

    def in_order(pair, carry):
        first = pair * 2
        bx, bz, by = coords(first)
        rows = pl.multiple_of(first * 8, 16)
        for p in range(2):
            if p == 0:
                one = (bx * NY + by) * NZ + bz
                two = one + NZ
            else:
                one = (by * NX + bx) * NZ + bz
                two = one + NX * NZ
            for g in range(2):
                wmat[g, pl.ds(rows, 16), p * W_HALF : (p + 1) * W_HALF] = jnp.concatenate(
                    [wbuf[p, one, g], wbuf[p, two, g]], axis=0
                )
        return carry

    lax.fori_loop(0, PEERS // 2, in_order, 0)

    def settle(step, carry):
        server = moved(me, step, sign)
        o_copy(me, server).wait_recv()
        l_copy(me, server).wait_recv()
        return carry

    lax.fori_loop(1, PEERS, settle, 0)

    def h_copy(t):
        return pltpu.make_async_remote_copy(
            src_ref=att.at[core, pl.ds(t * TILE, TILE)],
            dst_ref=att.at[core, pl.ds(t * TILE, TILE)],
            send_sem=h_send_sem.at[t],
            recv_sem=h_recv_sem.at[t],
            device_id={"head": 1 - core},
            device_id_type=pl.DeviceIdType.MESH,
        )

    for t in range(TILES):
        for h in range(HEADS):
            item = t * HEADS + h
            slots = [picked_ref[item * TOPK + j] for j in range(TOPK)]
            lses = [own_l[item]] + [recv_l[s] for s in slots]
            highest = functools.reduce(jnp.maximum, lses)
            factors = [jnp.exp2(v - highest) for v in lses]
            total = functools.reduce(jnp.add, factors)
            mixed = factors[0] * own_o[item]
            for f, s in zip(factors[1:], slots):
                mixed = mixed + f * recv_o[s].astype(jnp.float32)
            mixed = mixed / total
            att[core, t * TILE : (t + 1) * TILE, h * D_HEAD : (h + 1) * D_HEAD] = (
                mixed.T.astype(jnp.bfloat16)
            )
        h_copy(t).start()

    def project_own(chunk, carry):
        columns = pl.ds(pl.multiple_of(chunk * CHUNK, CHUNK), CHUNK)
        acc[:, columns] = jnp.dot(
            att[core], wmat[core, :, columns], preferred_element_type=jnp.float32
        )
        return carry

    lax.fori_loop(0, 2 * W_HALF // CHUNK, project_own, 0)
    for t in range(TILES):
        pltpu.make_async_remote_copy(
            src_ref=att.at[1 - core, pl.ds(t * TILE, TILE)],
            dst_ref=att.at[1 - core, pl.ds(t * TILE, TILE)],
            send_sem=h_send_sem.at[t],
            recv_sem=h_recv_sem.at[t],
            device_id={"head": 1 - core},
            device_id_type=pl.DeviceIdType.MESH,
        ).wait_recv()

    def project_other(chunk, carry):
        columns = pl.ds(pl.multiple_of(chunk * CHUNK, CHUNK), CHUNK)
        other = jnp.dot(
            att[1 - core], wmat[1 - core, :, columns], preferred_element_type=jnp.float32
        )
        out_ref[:, columns] = (acc[:, columns] + other).astype(jnp.bfloat16)
        return carry

    lax.fori_loop(0, 2 * W_HALF // CHUNK, project_other, 0)
    for t in range(TILES):
        h_copy(t).wait_send()
    for p in range(2):
        s_copy(p).wait_send()

    def drain(step, carry):
        target = moved(me, step, sign)
        q_copy(target, me).wait_send()
        source = moved(me, step, -sign)
        o_copy(source, me).wait_send()
        l_copy(source, me).wait_send()
        return carry

    lax.fori_loop(1, PEERS, drain, 0)
    for c in y_copies + z_copies + x_copies + w_started:
        c.wait_send()


def layer(wanted, picked, queries, keys, values, prefix_keys, prefix_values, weight):
    vmem = pl.BlockSpec(memory_space=pltpu.VMEM)
    smem = pl.BlockSpec(memory_space=pltpu.SMEM)
    slots = (PEERS, TILE, D_HEAD)
    width = HEADS * D_HEAD
    sem = pltpu.SemaphoreType.DMA
    return pl.pallas_call(
        layer_kernel,
        out_shape=jax.ShapeDtypeStruct((BLOCK, 2 * W_HALF), jnp.bfloat16),
        in_specs=[smem, smem, vmem, vmem, vmem, vmem, vmem, vmem, vmem],
        out_specs=vmem,
        scratch_shapes=[
            pltpu.VMEM((ITEMS, TILE, D_HEAD), jnp.bfloat16),
            pltpu.VMEM(slots, jnp.bfloat16),
            pltpu.VMEM(slots, jnp.bfloat16),
            pltpu.VMEM(slots, jnp.bfloat16),
            pltpu.VMEM((PEERS, 1, TILE), jnp.float32),
            pltpu.VMEM((PEERS, 1, TILE), jnp.float32),
            pltpu.VMEM((HEADS, BLOCK, D_HEAD), jnp.bfloat16),
            pltpu.VMEM((HEADS, D_HEAD, BLOCK), jnp.bfloat16),
            pltpu.VMEM((2, PEERS, 2, 8, W_HALF), jnp.bfloat16),
            pltpu.VMEM((2, width, 2 * W_HALF), jnp.bfloat16),
            pltpu.VMEM((2, BLOCK, width), jnp.bfloat16),
            pltpu.VMEM((BLOCK, 2 * W_HALF), jnp.float32),
            pltpu.VMEM((ITEMS, D_HEAD, TILE), jnp.float32),
            pltpu.VMEM((ITEMS, 1, TILE), jnp.float32),
            pltpu.VMEM((PEERS, 1, PEERS), jnp.int32),
            pltpu.SMEM((PEERS, 1, PEERS), jnp.int32),
            sem,
            sem((PEERS,)),
            sem((PEERS,)),
            sem((PEERS,)),
            sem((PEERS,)),
            sem((PEERS,)),
            sem((PEERS,)),
            sem((13,)),
            sem((13,)),
            sem((TILES,)),
            sem((TILES,)),
            sem((2,)),
            sem((2,)),
            sem((2, 15)),
            sem((2, 15)),
        ],
        compiler_params=pltpu.CompilerParams(
            collective_id=0, has_side_effects=True, vmem_limit_bytes=60 * 1024 * 1024
        ),
    )(wanted, picked, wanted[None], queries, keys, values, prefix_keys, prefix_values, weight)


def shards(queries, keys, values, prefix_keys, prefix_values, selected, out_weight):
    picked = selected.reshape(ITEMS * TOPK)
    matches = picked[None, :] == jnp.arange(PEERS, dtype=jnp.int32)[:, None]
    item_ids = jnp.arange(ITEMS * TOPK, dtype=jnp.int32) // TOPK
    wanted = jnp.sum(jnp.where(matches, item_ids[None, :], 0), axis=1)
    return layer(
        wanted, picked, queries, keys, values, prefix_keys, prefix_values, out_weight[0]
    )


def solution(mesh):
    return jax.shard_map(
        shards,
        mesh=mesh,
        in_specs=(
            P("ctx", "head"),
            P("ctx", "head"),
            P("ctx", "head"),
            P("ctx", "head"),
            P("ctx", "head"),
            P("head", "ctx", None, None),
            P("head", "ctx", None),
        ),
        out_specs=P("ctx", "head"),
        check_vma=False,
    )
```

```python
import functools
import math

import jax
import jax.numpy as jnp
from jax import lax
from jax.experimental import pallas as pl
from jax.experimental.pallas import tpu as pltpu
from jax.sharding import PartitionSpec as P

D_HEAD = 128
TILE = 128
BLOCK = 512
TOPK = 3
TILES = 4
HEADS = 8
ITEMS = TILES * HEADS
W_HALF = 1024
CHUNK = 512
TOGETHER = 3
NX, NZ, NY = 4, 8, 4
PEERS = NX * NZ * NY
PLANE = NX * NY
COLUMN = (0, -1, 1, -2, 2, -3, 3, 4)
SCALE2 = D_HEAD**-0.5 * math.log2(math.e)


def coords(index):
    return index // (NZ * NY), (index // NY) % NZ, index % NY


def place(x, z, y):
    return (x * NZ + z) * NY + y


def offset_of(step):
    dz = (step * 3) % NZ
    dy = (step // NZ) % NY
    dx = (step // (NZ * NY)) % NX
    return dx, dz, dy


def moved(me, step, sign):
    x, z, y = coords(me)
    dx, dz, dy = offset_of(step)
    return place((x + sign * dx + NX) % NX, (z + sign * dz + NZ) % NZ, (y + sign * dy + NY) % NY)


def attend(key_block, value_block_t, query, mask=None):
    scores = lax.dot_general(
        key_block, query, (((1,), (1,)), ((), ())), preferred_element_type=jnp.float32
    )
    scores = scores * SCALE2
    if mask is not None:
        scores = jnp.where(mask, scores, -jnp.inf)
    top = jnp.max(scores, axis=0, keepdims=True)
    weights = jnp.exp2(scores - top)
    total = jnp.sum(weights, axis=0, keepdims=True)
    out = lax.dot_general(
        value_block_t,
        weights.astype(jnp.bfloat16),
        (((1,), (0,)), ((), ())),
        preferred_element_type=jnp.float32,
    )
    return out / total, top + jnp.log2(total)


def layer_kernel(
    wanted_ref,
    picked_ref,
    wanted_row_ref,
    q_ref,
    k_ref,
    v_ref,
    pk_ref,
    pv_ref,
    w_ref,
    out_ref,
    items,
    up_one,
    up_two,
    down_one,
    down_two,
    onward,
    far,
    last,
    given,
    recv_q,
    recv_o,
    send_l,
    recv_l,
    kh,
    vt,
    wbuf,
    wmat,
    att,
    acc,
    own_o,
    own_l,
    table,
    column_s,
    table_s,
    table_sem,
    ring_send_sem,
    ring_recv_sem,
    q_send_sem,
    q_recv_sem,
    o_send_sem,
    o_recv_sem,
    l_send_sem,
    l_recv_sem,
    t_send_sem,
    t_recv_sem,
    h_send_sem,
    h_recv_sem,
    s_send_sem,
    s_recv_sem,
    w_send_sem,
    w_recv_sem,
):
    me = lax.axis_index("ctx")
    core = lax.axis_index("head")
    x, z, y = coords(me)
    sign = 1 - 2 * core
    near = ((up_one, up_two), (down_one, down_two))
    mesh = pl.DeviceIdType.MESH

    def depth(ahead):
        return (z + ahead + NZ) % NZ

    def remote(src, dst, send_sem, recv_sem, target):
        return pltpu.make_async_remote_copy(
            src_ref=src,
            dst_ref=dst,
            send_sem=send_sem,
            recv_sem=recv_sem,
            device_id={"ctx": target},
            device_id_type=mesh,
        )

    barrier = pltpu.get_barrier_semaphore()

    def greet(step, carry):
        pl.semaphore_signal(
            barrier, inc=1, device_id={"ctx": moved(me, step, 1)}, device_id_type=mesh
        )
        return carry

    lax.fori_loop(1, PEERS, greet, 0)
    pl.semaphore_signal(barrier, inc=1, device_id={"head": 1 - core}, device_id_type=mesh)

    for t in range(TILES):
        for h in range(HEADS):
            items[t * HEADS + h] = q_ref[
                t * TILE : (t + 1) * TILE, h * D_HEAD : (h + 1) * D_HEAD
            ]
    column_start = (x * NY + y) * NZ
    table[column_start + z] = wanted_row_ref[...]
    pl.semaphore_wait(barrier, PEERS)

    def ring(way, hop):
        if hop == 1:
            src, dst = items, near[way][0]
        elif hop == 2:
            src, dst = near[way][0], near[way][1]
        elif hop == 3:
            src, dst = onward.at[way], far.at[way]
        else:
            src, dst = far.at[way, pl.ds(PLANE, PLANE // 2)], last.at[
                pl.ds(way * (PLANE // 2), PLANE // 2)
            ]
        return remote(
            src,
            dst,
            ring_send_sem.at[way, hop - 1],
            ring_recv_sem.at[way, hop - 1],
            place(x, depth(1 - 2 * way), y),
        )

    started = []

    def start(copy):
        copy.start()
        started.append(copy)

    def w_major(p):
        return x if p == 0 else y

    def w_minor(p):
        return y if p == 0 else x

    def w_device(p, major, minor):
        return place(major, z, minor) if p == 0 else place(minor, z, major)

    def w_column(p):
        return (w_major(p) * NY + w_minor(p)) * NZ

    def w_copy(p, slot, first, blocks, target):
        return remote(
            wbuf.at[p, pl.ds(first, blocks)],
            wbuf.at[p, pl.ds(first, blocks)],
            w_send_sem.at[p, slot],
            w_recv_sem.at[p, slot],
            target,
        )

    def s_copy(p, group):
        columns = pl.multiple_of((1 - core) * 2 * W_HALF + p * W_HALF, W_HALF)
        return pltpu.make_async_remote_copy(
            src_ref=w_ref.at[:, pl.ds(columns, W_HALF)],
            dst_ref=wbuf.at[p, w_column(p) + z, group],
            send_sem=s_send_sem.at[p],
            recv_sem=s_recv_sem.at[p],
            device_id={"head": 1 - core},
            device_id_type=mesh,
        )

    def w_ways(hop, p):
        return (0, 1) if hop < 4 else (p,)

    def w_hop(hop):
        for p in range(2):
            for way in w_ways(hop, p):
                ahead = 1 - 2 * way
                block = w_column(p) + depth(-ahead * (hop - 1))
                start(w_copy(p, 2 * hop - 2 + way, block, 1, place(x, depth(ahead), y)))

    def w_hop_wait(hop):
        for p in range(2):
            for way in w_ways(hop, p):
                block = w_column(p) + depth(-(1 - 2 * way) * hop)
                w_copy(p, 2 * hop - 2 + way, block, 1, me).wait_recv()

    def w_line(p, level, ahead):
        if level == 0:
            minor = (w_minor(p) + ahead + 4) % 4
            return (w_major(p) * 4 + minor) * NZ, w_device(p, w_major(p), minor)
        major = (w_major(p) + ahead + 4) % 4
        return major * 4 * NZ, w_device(p, major, w_minor(p))

    def w_first(level):
        blocks = (NZ, 4 * NZ)[level]
        for p in range(2):
            first = w_line(p, level, 0)[0]
            start(w_copy(p, 8 + 4 * level, first, blocks, w_line(p, level, 1)[1]))
            start(w_copy(p, 9 + 4 * level, first, blocks, w_line(p, level, -1)[1]))

    def w_forward(level):
        blocks = (NZ, 4 * NZ)[level]
        half = blocks // 2
        for p in range(2):
            behind, ahead = w_line(p, level, -1), w_line(p, level, 1)
            w_copy(p, 8 + 4 * level, behind[0], blocks, me).wait_recv()
            start(w_copy(p, 10 + 4 * level, behind[0], half, ahead[1]))
            w_copy(p, 9 + 4 * level, ahead[0], blocks, me).wait_recv()
            start(w_copy(p, 11 + 4 * level, ahead[0] + half, half, behind[1]))

    def w_settle(level):
        half = (NZ, 4 * NZ)[level] // 2
        for p in range(2):
            opposite = w_line(p, level, 2)[0]
            w_copy(p, 10 + 4 * level, opposite, half, me).wait_recv()
            w_copy(p, 11 + 4 * level, opposite + half, half, me).wait_recv()

    def table_copy(slot, first, rows, target):
        return remote(
            table.at[pl.ds(first, rows)],
            table.at[pl.ds(first, rows)],
            t_send_sem.at[slot],
            t_recv_sem.at[slot],
            target,
        )

    for way in range(2):
        start(ring(way, 1))
    for p in range(2):
        s_copy(p, core).start()
        columns = pl.multiple_of(core * 2 * W_HALF + p * W_HALF, W_HALF)
        wbuf[p, w_column(p) + z, core] = w_ref[:, pl.ds(columns, W_HALF)]
    for d in range(1, NZ):
        start(table_copy(d - 1, column_start + z, 1, place(x, depth(d), y)))

    def in_plane(step, way):
        return (x + way * (step // NY) + NX) % NX, (y + way * (step % NY) + NY) % NY

    def q_copy(src, number, member, source, target):
        return remote(
            src, recv_q.at[source], q_send_sem.at[number, member], q_recv_sem.at[source], target
        )

    def hand_out(number, read, keep):
        source = place(x, depth(COLUMN[number]), y)

        def give(step, carry):
            tx, ty = in_plane(step, sign)
            member = tx * NY + ty
            target = place(tx, z, ty)
            q_copy(read(member, target), number, member, source, target).start()
            return carry

        lax.fori_loop(1, PLANE, give, 0)
        recv_q[source] = keep()

    def hand_out_tiles(number, tiles, row_of):
        def read(member, target):
            given[number, member] = tiles[row_of(target)]
            return given.at[number, member]

        hand_out(number, read, lambda: tiles[row_of(me)])

    def column_row(ahead):
        row = depth(ahead)
        return lambda target: column_s[row, 0, target]

    hand_out_tiles(0, items, lambda target: wanted_ref[target])

    for p in range(2):
        s_copy(p, 1 - core).wait_recv()
    w_hop(1)

    for d in range(1, NZ):
        table_copy(d - 1, column_start + depth(-d), 1, me).wait_recv()
    to_scalars = pltpu.make_async_copy(table.at[pl.ds(column_start, NZ)], column_s, table_sem)
    to_scalars.start()
    to_scalars.wait()
    for d in range(1, NY):
        start(table_copy(6 + d, column_start, NZ, place(x, z, (y + d) % NY)))

    def own_tile(t):
        keys_seen = (t + 1) * TILE
        row = lax.broadcasted_iota(jnp.int32, (keys_seen, TILE), 0)
        column = lax.broadcasted_iota(jnp.int32, (keys_seen, TILE), 1)
        mask = row <= column + t * TILE
        for h in range(HEADS):
            columns = slice(h * D_HEAD, (h + 1) * D_HEAD)
            out, lse = attend(
                k_ref[:keys_seen, columns],
                v_ref[:keys_seen, columns].T,
                q_ref[t * TILE : (t + 1) * TILE, columns],
                mask,
            )
            own_o[t * HEADS + h] = out
            own_l[t * HEADS + h] = lse

    for h in range(HEADS):
        columns = slice(h * D_HEAD, (h + 1) * D_HEAD)
        vt[h] = pv_ref[:, columns].T
        kh[h] = pk_ref[:, columns]
    for d in range(1, NY):
        table_copy(6 + d, (x * NY + (y - d + NY) % NY) * NZ, NZ, me).wait_recv()
    for d in range(1, NX):
        start(table_copy(9 + d, x * NY * NZ, NY * NZ, place((x + d) % NX, z, y)))
    for t in range(TILES):
        own_tile(t)
    for d in range(1, NX):
        table_copy(9 + d, (x - d + NX) % NX * NY * NZ, NY * NZ, me).wait_recv()
    to_scalars = pltpu.make_async_copy(table, table_s, table_sem)
    to_scalars.start()
    to_scalars.wait()

    def o_copy(target, slot):
        return remote(
            recv_q.at[target], recv_o.at[slot], o_send_sem.at[target], o_recv_sem.at[slot], target
        )

    def l_copy(target, slot):
        return remote(
            send_l.at[target], recv_l.at[slot], l_send_sem.at[target], l_recv_sem.at[slot], target
        )

    def answer(source):
        sx, sz, sy = coords(source)
        head = table_s[(sx * NY + sy) * NZ + sz, 0, me] % HEADS
        return attend(kh[head], vt[head], recv_q[source])

    def reply(source, found):
        recv_q[source] = found[0].astype(jnp.bfloat16)
        send_l[source] = found[1]
        o_copy(source, me).start()
        l_copy(source, me).start()

    def serve(number):
        ahead = COLUMN[number]
        plane = depth(ahead)
        if ahead == 0:
            out, lse = answer(me)
            recv_o[me] = out.astype(jnp.bfloat16)
            recv_l[me] = lse
        else:
            reply(place(x, plane, y), answer(place(x, plane, y)))

        def several(turn, carry):
            sources = []
            for j in range(TOGETHER):
                sx, sy = in_plane(1 + turn * TOGETHER + j, -sign)
                sources.append(place(sx, plane, sy))
            for source in sources:
                q_copy(given.at[0, 0], 0, 0, source, me).wait_recv()
            found = [answer(source) for source in sources]
            for source, one in zip(sources, found):
                reply(source, one)
            return carry

        lax.fori_loop(0, (PLANE - 1) // TOGETHER, several, 0)

    serve(0)

    for way in range(2):
        ring(way, 1).wait_recv()
        start(ring(way, 2))
    w_hop_wait(1)
    w_hop(2)
    for way in range(2):
        hand_out_tiles(1 + way, near[way][0], column_row(2 * way - 1))
    serve(1)
    serve(2)

    for way in range(2):
        ahead = 1 - 2 * way
        ring(way, 2).wait_recv()
        row_of = column_row(-2 * ahead)

        def build(member, carry, way=way, ahead=ahead, row_of=row_of):
            target = place(member // NY, depth(ahead), member % NY)
            onward[way, member] = near[way][1][row_of(target)]
            return carry

        def build_behind(member, carry, way=way, ahead=ahead, row_of=row_of):
            other = member + way * (PLANE // 2)
            target = place(other // NY, depth(2 * ahead), other % NY)
            onward[way, PLANE + member] = near[way][1][row_of(target)]
            return carry

        lax.fori_loop(0, PLANE, build, 0)
        lax.fori_loop(0, PLANE // 2, build_behind, 0)
        start(ring(way, 3))
    w_hop_wait(2)
    w_hop(3)
    for way in range(2):
        hand_out_tiles(3 + way, near[way][1], column_row(2 * (2 * way - 1)))
    serve(3)
    serve(4)

    here = x * NY + y
    for way in range(2):
        ring(way, 3).wait_recv()
        start(ring(way, 4))
    w_hop_wait(3)
    w_hop(4)
    for way in range(2):
        hand_out(
            5 + way, lambda member, target, way=way: far.at[way, member], lambda way=way: far[way, here]
        )
    serve(5)
    serve(6)

    for way in range(2):
        ring(way, 4).wait_recv()
    w_hop_wait(4)
    w_first(0)
    hand_out(7, lambda member, target: last.at[member], lambda: last[here])
    w_forward(0)
    serve(7)
    w_settle(0)
    w_first(1)
    w_forward(1)
    w_settle(1)

    def in_order(pair, carry):
        first = pair * 2
        bx, bz, by = coords(first)
        rows = pl.multiple_of(first * 8, 16)
        for p in range(2):
            if p == 0:
                one = (bx * NY + by) * NZ + bz
                two = one + NZ
            else:
                one = (by * NX + bx) * NZ + bz
                two = one + NX * NZ
            for g in range(2):
                wmat[g, pl.ds(rows, 16), p * W_HALF : (p + 1) * W_HALF] = jnp.concatenate(
                    [wbuf[p, one, g], wbuf[p, two, g]], axis=0
                )
        return carry

    lax.fori_loop(0, PEERS // 2, in_order, 0)

    def settle(step, carry):
        server = moved(me, step, sign)
        o_copy(me, server).wait_recv()
        l_copy(me, server).wait_recv()
        return carry

    lax.fori_loop(1, PEERS, settle, 0)

    def h_copy(t, group):
        return pltpu.make_async_remote_copy(
            src_ref=att.at[group, pl.ds(t * TILE, TILE)],
            dst_ref=att.at[group, pl.ds(t * TILE, TILE)],
            send_sem=h_send_sem.at[t],
            recv_sem=h_recv_sem.at[t],
            device_id={"head": 1 - core},
            device_id_type=mesh,
        )

    for t in range(TILES):
        for h in range(HEADS):
            item = t * HEADS + h
            slots = [picked_ref[item * TOPK + j] for j in range(TOPK)]
            lses = [own_l[item]] + [recv_l[s] for s in slots]
            highest = functools.reduce(jnp.maximum, lses)
            factors = [jnp.exp2(v - highest) for v in lses]
            total = functools.reduce(jnp.add, factors)
            mixed = factors[0] * own_o[item]
            for f, s in zip(factors[1:], slots):
                mixed = mixed + f * recv_o[s].astype(jnp.float32)
            mixed = mixed / total
            att[core, t * TILE : (t + 1) * TILE, h * D_HEAD : (h + 1) * D_HEAD] = mixed.T.astype(
                jnp.bfloat16
            )
        h_copy(t, core).start()

    def project_own(chunk, carry):
        columns = pl.ds(pl.multiple_of(chunk * CHUNK, CHUNK), CHUNK)
        acc[:, columns] = jnp.dot(
            att[core], wmat[core, :, columns], preferred_element_type=jnp.float32
        )
        return carry

    lax.fori_loop(0, 2 * W_HALF // CHUNK, project_own, 0)
    for t in range(TILES):
        h_copy(t, 1 - core).wait_recv()

    def project_other(chunk, carry):
        columns = pl.ds(pl.multiple_of(chunk * CHUNK, CHUNK), CHUNK)
        other = jnp.dot(
            att[1 - core], wmat[1 - core, :, columns], preferred_element_type=jnp.float32
        )
        out_ref[:, columns] = (acc[:, columns] + other).astype(jnp.bfloat16)
        return carry

    lax.fori_loop(0, 2 * W_HALF // CHUNK, project_other, 0)

    for t in range(TILES):
        h_copy(t, core).wait_send()
    for p in range(2):
        s_copy(p, core).wait_send()
    for number in range(NZ):

        def drain_slots(step, carry, number=number):
            tx, ty = in_plane(step, sign)
            q_copy(given.at[0, 0], number, tx * NY + ty, me, me).wait_send()
            return carry

        lax.fori_loop(1, PLANE, drain_slots, 0)

    def drain(step, carry):
        source = moved(me, step, -sign)
        o_copy(source, me).wait_send()
        l_copy(source, me).wait_send()
        return carry

    lax.fori_loop(1, PEERS, drain, 0)
    for copy in started:
        copy.wait_send()


def layer(wanted, picked, queries, keys, values, prefix_keys, prefix_values, weight):
    vmem = pl.BlockSpec(memory_space=pltpu.VMEM)
    smem = pl.BlockSpec(memory_space=pltpu.SMEM)
    slots = (PEERS, TILE, D_HEAD)
    width = HEADS * D_HEAD
    sem = pltpu.SemaphoreType.DMA
    return pl.pallas_call(
        layer_kernel,
        out_shape=jax.ShapeDtypeStruct((BLOCK, 2 * W_HALF), jnp.bfloat16),
        in_specs=[smem, smem, vmem, vmem, vmem, vmem, vmem, vmem, vmem],
        out_specs=vmem,
        scratch_shapes=[
            pltpu.VMEM((ITEMS, TILE, D_HEAD), jnp.bfloat16),
            pltpu.VMEM((ITEMS, TILE, D_HEAD), jnp.bfloat16),
            pltpu.VMEM((ITEMS, TILE, D_HEAD), jnp.bfloat16),
            pltpu.VMEM((ITEMS, TILE, D_HEAD), jnp.bfloat16),
            pltpu.VMEM((ITEMS, TILE, D_HEAD), jnp.bfloat16),
            pltpu.VMEM((2, 3 * PLANE // 2, TILE, D_HEAD), jnp.bfloat16),
            pltpu.VMEM((2, 3 * PLANE // 2, TILE, D_HEAD), jnp.bfloat16),
            pltpu.VMEM((PLANE, TILE, D_HEAD), jnp.bfloat16),
            pltpu.VMEM((5, PLANE, TILE, D_HEAD), jnp.bfloat16),
            pltpu.VMEM(slots, jnp.bfloat16),
            pltpu.VMEM(slots, jnp.bfloat16),
            pltpu.VMEM((PEERS, 1, TILE), jnp.float32),
            pltpu.VMEM((PEERS, 1, TILE), jnp.float32),
            pltpu.VMEM((HEADS, BLOCK, D_HEAD), jnp.bfloat16),
            pltpu.VMEM((HEADS, D_HEAD, BLOCK), jnp.bfloat16),
            pltpu.VMEM((2, PEERS, 2, 8, W_HALF), jnp.bfloat16),
            pltpu.VMEM((2, width, 2 * W_HALF), jnp.bfloat16),
            pltpu.VMEM((2, BLOCK, width), jnp.bfloat16),
            pltpu.VMEM((BLOCK, 2 * W_HALF), jnp.float32),
            pltpu.VMEM((ITEMS, D_HEAD, TILE), jnp.float32),
            pltpu.VMEM((ITEMS, 1, TILE), jnp.float32),
            pltpu.VMEM((PEERS, 1, PEERS), jnp.int32),
            pltpu.SMEM((NZ, 1, PEERS), jnp.int32),
            pltpu.SMEM((PEERS, 1, PEERS), jnp.int32),
            sem,
            sem((2, 4)),
            sem((2, 4)),
            sem((NZ, PLANE)),
            sem((PEERS,)),
            sem((PEERS,)),
            sem((PEERS,)),
            sem((PEERS,)),
            sem((PEERS,)),
            sem((13,)),
            sem((13,)),
            sem((TILES,)),
            sem((TILES,)),
            sem((2,)),
            sem((2,)),
            sem((2, 16)),
            sem((2, 16)),
        ],
        compiler_params=pltpu.CompilerParams(
            collective_id=0, has_side_effects=True, vmem_limit_bytes=60 * 1024 * 1024
        ),
    )(wanted, picked, wanted[None], queries, keys, values, prefix_keys, prefix_values, weight)


def shards(queries, keys, values, prefix_keys, prefix_values, selected, out_weight):
    picked = selected.reshape(ITEMS * TOPK)
    matches = picked[None, :] == jnp.arange(PEERS, dtype=jnp.int32)[:, None]
    item_ids = jnp.arange(ITEMS * TOPK, dtype=jnp.int32) // TOPK
    wanted = jnp.sum(jnp.where(matches, item_ids[None, :], 0), axis=1)
    return layer(
        wanted, picked, queries, keys, values, prefix_keys, prefix_values, out_weight[0]
    )


def solution(mesh):
    return jax.shard_map(
        shards,
        mesh=mesh,
        in_specs=(
            P("ctx", "head"),
            P("ctx", "head"),
            P("ctx", "head"),
            P("ctx", "head"),
            P("ctx", "head"),
            P("head", "ctx", None, None),
            P("head", "ctx", None),
        ),
        out_specs=P("ctx", "head"),
        check_vma=False,
    )
```

```python
import functools
import math

import jax
import jax.numpy as jnp
from jax import lax
from jax.experimental import pallas as pl
from jax.experimental.pallas import tpu as pltpu
from jax.sharding import PartitionSpec as P

D_HEAD = 128
TILE = 128
BLOCK = 512
TOPK = 3
TILES = 4
HEADS = 8
ITEMS = TILES * HEADS
W_HALF = 1024
CHUNK = 512
NX, NZ, NY = 4, 8, 4
PEERS = NX * NZ * NY
SCALE2 = D_HEAD**-0.5 * math.log2(math.e)


def coords(index):
    return index // (NZ * NY), (index // NY) % NZ, index % NY


def place(x, z, y):
    return (x * NZ + z) * NY + y


def offset_of(step):
    dz = (step * 3) % NZ
    dy = (step // NZ) % NY
    dx = (step // (NZ * NY)) % NX
    return dx, dz, dy


def moved(me, step, sign):
    x, z, y = coords(me)
    dx, dz, dy = offset_of(step)
    return place((x + sign * dx + NX) % NX, (z + sign * dz + NZ) % NZ, (y + sign * dy + NY) % NY)


def attend(key_block, value_block_t, query, mask=None):
    scores = lax.dot_general(
        key_block, query, (((1,), (1,)), ((), ())), preferred_element_type=jnp.float32
    )
    scores = scores * SCALE2
    if mask is not None:
        scores = jnp.where(mask, scores, -jnp.inf)
    top = jnp.max(scores, axis=0, keepdims=True)
    weights = jnp.exp2(scores - top)
    total = jnp.sum(weights, axis=0, keepdims=True)
    out = lax.dot_general(
        value_block_t,
        weights.astype(jnp.bfloat16),
        (((1,), (0,)), ((), ())),
        preferred_element_type=jnp.float32,
    )
    return out * (1.0 / total), top + jnp.log2(total)


def layer_kernel(
    wanted_ref,
    picked_ref,
    wanted_row_ref,
    q_ref,
    k_ref,
    v_ref,
    pk_ref,
    pv_ref,
    w_ref,
    out_ref,
    items,
    send_q,
    recv_q,
    recv_o,
    send_l,
    recv_l,
    kh,
    vt,
    wbuf,
    wmat,
    att,
    acc,
    own_o,
    own_l,
    table,
    table_s,
    table_sem,
    q_send_sem,
    q_recv_sem,
    o_send_sem,
    o_recv_sem,
    l_send_sem,
    l_recv_sem,
    t_send_sem,
    t_recv_sem,
    h_send_sem,
    h_recv_sem,
    s_send_sem,
    s_recv_sem,
    w_send_sem,
    w_recv_sem,
):
    me = lax.axis_index("ctx")
    core = lax.axis_index("head")
    x, z, y = coords(me)
    sign = 1 - 2 * core

    barrier = pltpu.get_barrier_semaphore()

    def greet(step, carry):
        pl.semaphore_signal(
            barrier,
            inc=1,
            device_id={"ctx": moved(me, step, 1)},
            device_id_type=pl.DeviceIdType.MESH,
        )
        return carry

    lax.fori_loop(1, PEERS, greet, 0)
    pl.semaphore_signal(
        barrier, inc=1, device_id={"head": 1 - core}, device_id_type=pl.DeviceIdType.MESH
    )

    for t in range(TILES):
        for h in range(HEADS):
            items[t * HEADS + h] = q_ref[
                t * TILE : (t + 1) * TILE, h * D_HEAD : (h + 1) * D_HEAD
            ]
    table[me] = wanted_row_ref[...]
    pl.semaphore_wait(barrier, PEERS)

    def table_copy(slot, rows, start, target):
        return pltpu.make_async_remote_copy(
            src_ref=table.at[pl.ds(start, rows)],
            dst_ref=table.at[pl.ds(start, rows)],
            send_sem=t_send_sem.at[slot],
            recv_sem=t_recv_sem.at[slot],
            device_id={"ctx": target},
            device_id_type=pl.DeviceIdType.MESH,
        )

    def w_major(p):
        return x if p == 0 else y

    def w_minor(p):
        return y if p == 0 else x

    def w_device(p, major, minor, depth):
        return place(major, depth, minor) if p == 0 else place(minor, depth, major)

    def w_pos(p):
        return (w_major(p) * NY + w_minor(p)) * NZ + z

    def w_copy(p, slot, start, blocks, target):
        return pltpu.make_async_remote_copy(
            src_ref=wbuf.at[p, pl.ds(start, blocks)],
            dst_ref=wbuf.at[p, pl.ds(start, blocks)],
            send_sem=w_send_sem.at[p, slot],
            recv_sem=w_recv_sem.at[p, slot],
            device_id={"ctx": target},
            device_id_type=pl.DeviceIdType.MESH,
        )

    def s_copy(p):
        columns = pl.multiple_of((1 - core) * 2 * W_HALF + p * W_HALF, W_HALF)
        return pltpu.make_async_remote_copy(
            src_ref=w_ref.at[:, pl.ds(columns, W_HALF)],
            dst_ref=wbuf.at[p, w_pos(p), core],
            send_sem=s_send_sem.at[p],
            recv_sem=s_recv_sem.at[p],
            device_id={"head": 1 - core},
            device_id_type=pl.DeviceIdType.MESH,
        )

    w_started = []

    def w_send(p, slot, start, blocks, target):
        c = w_copy(p, slot, start, blocks, target)
        c.start()
        w_started.append(c)

    def w_line(p, level, ahead):
        if level == 0:
            minor = (w_minor(p) + ahead + 4) % 4
            return (w_major(p) * 4 + minor) * NZ, w_device(p, w_major(p), minor, z)
        major = (w_major(p) + ahead + 4) % 4
        return major * 4 * NZ, w_device(p, major, w_minor(p), z)

    def w_first(level):
        blocks = (NZ, 4 * NZ)[level]
        for p in range(2):
            start = w_line(p, level, 0)[0]
            w_send(p, 8 + 4 * level, start, blocks, w_line(p, level, 1)[1])
            w_send(p, 9 + 4 * level, start, blocks, w_line(p, level, -1)[1])

    def w_forward(level):
        blocks = (NZ, 4 * NZ)[level]
        half = blocks // 2
        for p in range(2):
            behind, ahead = w_line(p, level, -1), w_line(p, level, 1)
            w_copy(p, 8 + 4 * level, behind[0], blocks, me).wait_recv()
            w_send(p, 10 + 4 * level, behind[0], half, ahead[1])
            w_copy(p, 9 + 4 * level, ahead[0], blocks, me).wait_recv()
            w_send(p, 11 + 4 * level, ahead[0] + half, half, behind[1])

    def w_settle(level):
        half = (NZ, 4 * NZ)[level] // 2
        for p in range(2):
            opposite = w_line(p, level, 2)[0]
            w_copy(p, 10 + 4 * level, opposite, half, me).wait_recv()
            w_copy(p, 11 + 4 * level, opposite + half, half, me).wait_recv()

    for p in range(2):
        s_copy(p).start()
        columns = pl.multiple_of(core * 2 * W_HALF + p * W_HALF, W_HALF)
        wbuf[p, w_pos(p), core] = w_ref[:, pl.ds(columns, W_HALF)]

    y_copies = [table_copy(d - 1, 1, me, place(x, z, (y + d) % NY)) for d in range(1, NY)]
    for c in y_copies:
        c.start()

    def w_ways(hop, p):
        return (0, 1) if hop < 4 else (p,)

    def w_block(p, ahead):
        return w_pos(p) - z + (z + ahead + NZ) % NZ

    def w_hop(hop):
        for p in range(2):
            for way in w_ways(hop, p):
                ahead = 1 - 2 * way
                w_send(
                    p,
                    2 * hop - 2 + way,
                    w_block(p, -ahead * (hop - 1)),
                    1,
                    place(x, (z + ahead + NZ) % NZ, y),
                )

    def w_hop_wait(hop):
        for p in range(2):
            for way in w_ways(hop, p):
                block = w_block(p, -(1 - 2 * way) * hop)
                w_copy(p, 2 * hop - 2 + way, block, 1, me).wait_recv()

    def q_copy(target, slot):
        return pltpu.make_async_remote_copy(
            src_ref=send_q.at[target],
            dst_ref=recv_q.at[slot],
            send_sem=q_send_sem.at[target],
            recv_sem=q_recv_sem.at[slot],
            device_id={"ctx": target},
            device_id_type=pl.DeviceIdType.MESH,
        )

    def send_query(step, carry):
        target = moved(me, step, sign)
        send_q[target] = items[wanted_ref[target]]
        q_copy(target, me).start()
        return carry

    lax.fori_loop(1, 17, send_query, 0)
    for p in range(2):
        pltpu.make_async_remote_copy(
            src_ref=w_ref.at[:, pl.ds(0, W_HALF)],
            dst_ref=wbuf.at[p, w_pos(p), 1 - core],
            send_sem=s_send_sem.at[p],
            recv_sem=s_recv_sem.at[p],
            device_id={"head": 1 - core},
            device_id_type=pl.DeviceIdType.MESH,
        ).wait_recv()
    w_hop(1)
    for d in range(1, NY):
        table_copy(d - 1, 1, place(x, z, (y - d + NY) % NY), me).wait_recv()
    z_copies = [
        table_copy(2 + d, NY, place(x, z, 0), place(x, (z + d) % NZ, y)) for d in range(1, NZ)
    ]
    for c in z_copies:
        c.start()
    lax.fori_loop(17, 49, send_query, 0)
    w_hop_wait(1)
    w_hop(2)
    for d in range(1, NZ):
        table_copy(2 + d, NY, place(x, (z - d + NZ) % NZ, 0), me).wait_recv()
    x_copies = [
        table_copy(9 + d, NZ * NY, place(x, 0, 0), place((x + d) % NX, z, y))
        for d in range(1, NX)
    ]
    for c in x_copies:
        c.start()
    lax.fori_loop(49, PEERS, send_query, 0)

    for t in range(TILES):
        depth = (t + 1) * TILE
        row = lax.broadcasted_iota(jnp.int32, (depth, TILE), 0)
        column = lax.broadcasted_iota(jnp.int32, (depth, TILE), 1)
        mask = row <= column + t * TILE
        for h in range(HEADS):
            columns = slice(h * D_HEAD, (h + 1) * D_HEAD)
            out, lse = attend(
                k_ref[:depth, columns],
                v_ref[:depth, columns].T,
                q_ref[t * TILE : (t + 1) * TILE, columns],
                mask,
            )
            own_o[t * HEADS + h] = out
            own_l[t * HEADS + h] = lse
        if t == 1:
            w_hop_wait(2)
            w_hop(3)
        elif t == 2:
            w_hop_wait(3)
            w_hop(4)
    for h in range(HEADS):
        columns = slice(h * D_HEAD, (h + 1) * D_HEAD)
        vt[h] = pv_ref[:, columns].T
        kh[h] = pk_ref[:, columns]
    w_hop_wait(4)
    w_first(0)

    for d in range(1, NX):
        table_copy(9 + d, NZ * NY, place((x - d + NX) % NX, 0, 0), me).wait_recv()
    to_scalars = pltpu.make_async_copy(table, table_s, table_sem)
    to_scalars.start()
    to_scalars.wait()

    def o_copy(target, slot):
        return pltpu.make_async_remote_copy(
            src_ref=recv_q.at[target],
            dst_ref=recv_o.at[slot],
            send_sem=o_send_sem.at[target],
            recv_sem=o_recv_sem.at[slot],
            device_id={"ctx": target},
            device_id_type=pl.DeviceIdType.MESH,
        )

    def l_copy(target, slot):
        return pltpu.make_async_remote_copy(
            src_ref=send_l.at[target],
            dst_ref=recv_l.at[slot],
            send_sem=l_send_sem.at[target],
            recv_sem=l_recv_sem.at[slot],
            device_id={"ctx": target},
            device_id_type=pl.DeviceIdType.MESH,
        )

    def answer(source, query):
        head = table_s[source, 0, me] % HEADS
        return attend(kh[head], vt[head], query)

    out, lse = answer(me, items[wanted_ref[me]])
    recv_o[me] = out.astype(jnp.bfloat16)
    recv_l[me] = lse

    def serve(step, carry):
        source = moved(me, step, -sign)
        q_copy(me, source).wait_recv()
        out, lse = answer(source, recv_q[source])
        recv_q[source] = out.astype(jnp.bfloat16)
        send_l[source] = lse
        o_copy(source, me).start()
        l_copy(source, me).start()
        return carry

    lax.fori_loop(1, 9, serve, 0)
    w_forward(0)
    lax.fori_loop(9, 17, serve, 0)
    w_settle(0)
    w_first(1)
    lax.fori_loop(17, 80, serve, 0)
    w_forward(1)
    lax.fori_loop(80, PEERS, serve, 0)

    w_settle(1)

    def in_order(pair, carry):
        first = pair * 2
        bx, bz, by = coords(first)
        rows = pl.multiple_of(first * 8, 16)
        for p in range(2):
            if p == 0:
                one = (bx * NY + by) * NZ + bz
                two = one + NZ
            else:
                one = (by * NX + bx) * NZ + bz
                two = one + NX * NZ
            for g in range(2):
                wmat[g, pl.ds(rows, 16), p * W_HALF : (p + 1) * W_HALF] = jnp.concatenate(
                    [wbuf[p, one, g], wbuf[p, two, g]], axis=0
                )
        return carry

    lax.fori_loop(0, PEERS // 2, in_order, 0)

    def settle(step, carry):
        server = moved(me, step, sign)
        o_copy(me, server).wait_recv()
        l_copy(me, server).wait_recv()
        return carry

    lax.fori_loop(1, PEERS, settle, 0)

    def h_copy(t):
        return pltpu.make_async_remote_copy(
            src_ref=att.at[core, pl.ds(t * TILE, TILE)],
            dst_ref=att.at[core, pl.ds(t * TILE, TILE)],
            send_sem=h_send_sem.at[t],
            recv_sem=h_recv_sem.at[t],
            device_id={"head": 1 - core},
            device_id_type=pl.DeviceIdType.MESH,
        )

    for t in range(TILES):
        for h in range(HEADS):
            item = t * HEADS + h
            slots = [picked_ref[item * TOPK + j] for j in range(TOPK)]
            lses = [own_l[item]] + [recv_l[s] for s in slots]
            highest = functools.reduce(jnp.maximum, lses)
            factors = [jnp.exp2(v - highest) for v in lses]
            total = functools.reduce(jnp.add, factors)
            factors = [f * (1.0 / total) for f in factors]
            mixed = factors[0] * own_o[item]
            for f, s in zip(factors[1:], slots):
                mixed = mixed + f * recv_o[s].astype(jnp.float32)
            att[core, t * TILE : (t + 1) * TILE, h * D_HEAD : (h + 1) * D_HEAD] = (
                mixed.T.astype(jnp.bfloat16)
            )
        h_copy(t).start()

    def project_own(chunk, carry):
        columns = pl.ds(pl.multiple_of(chunk * CHUNK, CHUNK), CHUNK)
        acc[:, columns] = jnp.dot(
            att[core], wmat[core, :, columns], preferred_element_type=jnp.float32
        )
        return carry

    lax.fori_loop(0, 2 * W_HALF // CHUNK, project_own, 0)
    for t in range(TILES):
        pltpu.make_async_remote_copy(
            src_ref=att.at[1 - core, pl.ds(t * TILE, TILE)],
            dst_ref=att.at[1 - core, pl.ds(t * TILE, TILE)],
            send_sem=h_send_sem.at[t],
            recv_sem=h_recv_sem.at[t],
            device_id={"head": 1 - core},
            device_id_type=pl.DeviceIdType.MESH,
        ).wait_recv()

    def project_other(chunk, carry):
        columns = pl.ds(pl.multiple_of(chunk * CHUNK, CHUNK), CHUNK)
        other = jnp.dot(
            att[1 - core], wmat[1 - core, :, columns], preferred_element_type=jnp.float32
        )
        out_ref[:, columns] = (acc[:, columns] + other).astype(jnp.bfloat16)
        return carry

    lax.fori_loop(0, 2 * W_HALF // CHUNK, project_other, 0)
    for t in range(TILES):
        h_copy(t).wait_send()
    for p in range(2):
        s_copy(p).wait_send()

    def drain(step, carry):
        target = moved(me, step, sign)
        q_copy(target, me).wait_send()
        source = moved(me, step, -sign)
        o_copy(source, me).wait_send()
        l_copy(source, me).wait_send()
        return carry

    lax.fori_loop(1, PEERS, drain, 0)
    for c in y_copies + z_copies + x_copies + w_started:
        c.wait_send()


def layer(wanted, picked, queries, keys, values, prefix_keys, prefix_values, weight):
    vmem = pl.BlockSpec(memory_space=pltpu.VMEM)
    smem = pl.BlockSpec(memory_space=pltpu.SMEM)
    slots = (PEERS, TILE, D_HEAD)
    width = HEADS * D_HEAD
    sem = pltpu.SemaphoreType.DMA
    return pl.pallas_call(
        layer_kernel,
        out_shape=jax.ShapeDtypeStruct((BLOCK, 2 * W_HALF), jnp.bfloat16),
        in_specs=[smem, smem, vmem, vmem, vmem, vmem, vmem, vmem, vmem],
        out_specs=vmem,
        scratch_shapes=[
            pltpu.VMEM((ITEMS, TILE, D_HEAD), jnp.bfloat16),
            pltpu.VMEM(slots, jnp.bfloat16),
            pltpu.VMEM(slots, jnp.bfloat16),
            pltpu.VMEM(slots, jnp.bfloat16),
            pltpu.VMEM((PEERS, 1, TILE), jnp.float32),
            pltpu.VMEM((PEERS, 1, TILE), jnp.float32),
            pltpu.VMEM((HEADS, BLOCK, D_HEAD), jnp.bfloat16),
            pltpu.VMEM((HEADS, D_HEAD, BLOCK), jnp.bfloat16),
            pltpu.VMEM((2, PEERS, 2, 8, W_HALF), jnp.bfloat16),
            pltpu.VMEM((2, width, 2 * W_HALF), jnp.bfloat16),
            pltpu.VMEM((2, BLOCK, width), jnp.bfloat16),
            pltpu.VMEM((BLOCK, 2 * W_HALF), jnp.float32),
            pltpu.VMEM((ITEMS, D_HEAD, TILE), jnp.float32),
            pltpu.VMEM((ITEMS, 1, TILE), jnp.float32),
            pltpu.VMEM((PEERS, 1, PEERS), jnp.int32),
            pltpu.SMEM((PEERS, 1, PEERS), jnp.int32),
            sem,
            sem((PEERS,)),
            sem((PEERS,)),
            sem((PEERS,)),
            sem((PEERS,)),
            sem((PEERS,)),
            sem((PEERS,)),
            sem((13,)),
            sem((13,)),
            sem((TILES,)),
            sem((TILES,)),
            sem((2,)),
            sem((2,)),
            sem((2, 16)),
            sem((2, 16)),
        ],
        compiler_params=pltpu.CompilerParams(
            collective_id=0, has_side_effects=True, vmem_limit_bytes=60 * 1024 * 1024
        ),
    )(wanted, picked, wanted[None], queries, keys, values, prefix_keys, prefix_values, weight)


def shards(queries, keys, values, prefix_keys, prefix_values, selected, out_weight):
    picked = selected.reshape(ITEMS * TOPK)
    matches = picked[None, :] == jnp.arange(PEERS, dtype=jnp.int32)[:, None]
    item_ids = jnp.arange(ITEMS * TOPK, dtype=jnp.int32) // TOPK
    wanted = jnp.sum(jnp.where(matches, item_ids[None, :], 0), axis=1)
    return layer(
        wanted, picked, queries, keys, values, prefix_keys, prefix_values, out_weight[0]
    )


def solution(mesh):
    return jax.shard_map(
        shards,
        mesh=mesh,
        in_specs=(
            P("ctx", "head"),
            P("ctx", "head"),
            P("ctx", "head"),
            P("ctx", "head"),
            P("ctx", "head"),
            P("head", "ctx", None, None),
            P("head", "ctx", None),
        ),
        out_specs=P("ctx", "head"),
        check_vma=False,
    )
```

```python
import functools
import math

import jax
import jax.numpy as jnp
from jax import lax
from jax.experimental import pallas as pl
from jax.experimental.pallas import tpu as pltpu
from jax.sharding import PartitionSpec as P

D_HEAD = 128
TILE = 128
BLOCK = 512
TOPK = 3
TILES = 4
HEADS = 8
ITEMS = TILES * HEADS
W_HALF = 1024
CHUNK = 512
NX, NZ, NY = 4, 8, 4
PEERS = NX * NZ * NY
SCALE2 = D_HEAD**-0.5 * math.log2(math.e)


def coords(index):
    return index // (NZ * NY), (index // NY) % NZ, index % NY


def place(x, z, y):
    return (x * NZ + z) * NY + y


def offset_of(step):
    dz = (step * 3) % NZ
    dy = (step // NZ) % NY
    dx = (step // (NZ * NY)) % NX
    return dx, dz, dy


def moved(me, step, sign):
    x, z, y = coords(me)
    dx, dz, dy = offset_of(step)
    return place((x + sign * dx + NX) % NX, (z + sign * dz + NZ) % NZ, (y + sign * dy + NY) % NY)


def attend(key_block, value_block_t, query, mask=None):
    scores = lax.dot_general(
        key_block, query, (((1,), (1,)), ((), ())), preferred_element_type=jnp.float32
    )
    scores = scores * SCALE2
    if mask is not None:
        scores = jnp.where(mask, scores, -jnp.inf)
    top = jnp.max(scores, axis=0, keepdims=True)
    weights = jnp.exp2(scores - top)
    total = jnp.sum(weights, axis=0, keepdims=True)
    out = lax.dot_general(
        value_block_t,
        weights.astype(jnp.bfloat16),
        (((1,), (0,)), ((), ())),
        preferred_element_type=jnp.float32,
    )
    return out * (1.0 / total), top + jnp.log2(total)


def layer_kernel(
    wanted_ref,
    picked_ref,
    wanted_row_ref,
    q_ref,
    k_ref,
    v_ref,
    pk_ref,
    pv_ref,
    w_ref,
    out_ref,
    items,
    send_q,
    recv_q,
    recv_o,
    send_l,
    recv_l,
    kh,
    vt,
    wbuf,
    wmat,
    att,
    acc,
    own_o,
    own_l,
    table,
    table_s,
    table_sem,
    q_send_sem,
    q_recv_sem,
    o_send_sem,
    o_recv_sem,
    l_send_sem,
    l_recv_sem,
    t_send_sem,
    t_recv_sem,
    h_send_sem,
    h_recv_sem,
    s_send_sem,
    s_recv_sem,
    w_send_sem,
    w_recv_sem,
):
    me = lax.axis_index("ctx")
    core = lax.axis_index("head")
    x, z, y = coords(me)
    sign = 1 - 2 * core

    barrier = pltpu.get_barrier_semaphore()

    def greet(step, carry):
        pl.semaphore_signal(
            barrier,
            inc=1,
            device_id={"ctx": moved(me, step, 1)},
            device_id_type=pl.DeviceIdType.MESH,
        )
        return carry

    lax.fori_loop(1, PEERS, greet, 0)
    pl.semaphore_signal(
        barrier, inc=1, device_id={"head": 1 - core}, device_id_type=pl.DeviceIdType.MESH
    )

    for t in range(TILES):
        for h in range(HEADS):
            items[t * HEADS + h] = q_ref[
                t * TILE : (t + 1) * TILE, h * D_HEAD : (h + 1) * D_HEAD
            ]
    table[me] = wanted_row_ref[...]
    pl.semaphore_wait(barrier, PEERS)

    def table_copy(slot, rows, start, target):
        return pltpu.make_async_remote_copy(
            src_ref=table.at[pl.ds(start, rows)],
            dst_ref=table.at[pl.ds(start, rows)],
            send_sem=t_send_sem.at[slot],
            recv_sem=t_recv_sem.at[slot],
            device_id={"ctx": target},
            device_id_type=pl.DeviceIdType.MESH,
        )

    def w_major(p):
        return x if p == 0 else y

    def w_minor(p):
        return y if p == 0 else x

    def w_device(p, major, minor, depth):
        return place(major, depth, minor) if p == 0 else place(minor, depth, major)

    def w_pos(p):
        return (w_major(p) * NY + w_minor(p)) * NZ + z

    def w_copy(p, slot, start, blocks, target):
        return pltpu.make_async_remote_copy(
            src_ref=wbuf.at[p, pl.ds(start, blocks)],
            dst_ref=wbuf.at[p, pl.ds(start, blocks)],
            send_sem=w_send_sem.at[p, slot],
            recv_sem=w_recv_sem.at[p, slot],
            device_id={"ctx": target},
            device_id_type=pl.DeviceIdType.MESH,
        )

    def s_copy(p):
        columns = pl.multiple_of((1 - core) * 2 * W_HALF + p * W_HALF, W_HALF)
        return pltpu.make_async_remote_copy(
            src_ref=w_ref.at[:, pl.ds(columns, W_HALF)],
            dst_ref=wbuf.at[p, w_pos(p), core],
            send_sem=s_send_sem.at[p],
            recv_sem=s_recv_sem.at[p],
            device_id={"head": 1 - core},
            device_id_type=pl.DeviceIdType.MESH,
        )

    w_started = []

    def w_send(p, slot, start, blocks, target):
        c = w_copy(p, slot, start, blocks, target)
        c.start()
        w_started.append(c)

    def w_line(p, level, ahead):
        if level == 0:
            minor = (w_minor(p) + ahead + 4) % 4
            return (w_major(p) * 4 + minor) * NZ, w_device(p, w_major(p), minor, z)
        major = (w_major(p) + ahead + 4) % 4
        return major * 4 * NZ, w_device(p, major, w_minor(p), z)

    def w_first(level):
        blocks = (NZ, 4 * NZ)[level]
        for p in range(2):
            start = w_line(p, level, 0)[0]
            w_send(p, 8 + 4 * level, start, blocks, w_line(p, level, 1)[1])
            w_send(p, 9 + 4 * level, start, blocks, w_line(p, level, -1)[1])

    def w_forward(level):
        blocks = (NZ, 4 * NZ)[level]
        half = blocks // 2
        for p in range(2):
            behind, ahead = w_line(p, level, -1), w_line(p, level, 1)
            w_copy(p, 8 + 4 * level, behind[0], blocks, me).wait_recv()
            w_send(p, 10 + 4 * level, behind[0], half, ahead[1])
            w_copy(p, 9 + 4 * level, ahead[0], blocks, me).wait_recv()
            w_send(p, 11 + 4 * level, ahead[0] + half, half, behind[1])

    def w_settle(level):
        half = (NZ, 4 * NZ)[level] // 2
        for p in range(2):
            opposite = w_line(p, level, 2)[0]
            w_copy(p, 10 + 4 * level, opposite, half, me).wait_recv()
            w_copy(p, 11 + 4 * level, opposite + half, half, me).wait_recv()

    for p in range(2):
        s_copy(p).start()
        columns = pl.multiple_of(core * 2 * W_HALF + p * W_HALF, W_HALF)
        wbuf[p, w_pos(p), core] = w_ref[:, pl.ds(columns, W_HALF)]

    y_copies = [table_copy(d - 1, 1, me, place(x, z, (y + d) % NY)) for d in range(1, NY)]
    for c in y_copies:
        c.start()

    def w_ways(hop, p):
        return (0, 1) if hop < 4 else (p,)

    def w_block(p, ahead):
        return w_pos(p) - z + (z + ahead + NZ) % NZ

    def w_hop(hop):
        for p in range(2):
            for way in w_ways(hop, p):
                ahead = 1 - 2 * way
                w_send(
                    p,
                    2 * hop - 2 + way,
                    w_block(p, -ahead * (hop - 1)),
                    1,
                    place(x, (z + ahead + NZ) % NZ, y),
                )

    def w_hop_wait(hop):
        for p in range(2):
            for way in w_ways(hop, p):
                block = w_block(p, -(1 - 2 * way) * hop)
                w_copy(p, 2 * hop - 2 + way, block, 1, me).wait_recv()

    def q_copy(target, slot):
        return pltpu.make_async_remote_copy(
            src_ref=send_q.at[target],
            dst_ref=recv_q.at[slot],
            send_sem=q_send_sem.at[target],
            recv_sem=q_recv_sem.at[slot],
            device_id={"ctx": target},
            device_id_type=pl.DeviceIdType.MESH,
        )

    def send_query(step, carry):
        target = moved(me, step, sign)
        send_q[target] = items[wanted_ref[target]]
        q_copy(target, me).start()
        return carry

    lax.fori_loop(1, 17, send_query, 0)
    for p in range(2):
        pltpu.make_async_remote_copy(
            src_ref=w_ref.at[:, pl.ds(0, W_HALF)],
            dst_ref=wbuf.at[p, w_pos(p), 1 - core],
            send_sem=s_send_sem.at[p],
            recv_sem=s_recv_sem.at[p],
            device_id={"head": 1 - core},
            device_id_type=pl.DeviceIdType.MESH,
        ).wait_recv()
    w_hop(1)
    for d in range(1, NY):
        table_copy(d - 1, 1, place(x, z, (y - d + NY) % NY), me).wait_recv()
    z_copies = [
        table_copy(2 + d, NY, place(x, z, 0), place(x, (z + d) % NZ, y)) for d in range(1, NZ)
    ]
    for c in z_copies:
        c.start()
    lax.fori_loop(17, 49, send_query, 0)
    w_hop_wait(1)
    w_hop(2)
    for d in range(1, NZ):
        table_copy(2 + d, NY, place(x, (z - d + NZ) % NZ, 0), me).wait_recv()
    x_copies = [
        table_copy(9 + d, NZ * NY, place(x, 0, 0), place((x + d) % NX, z, y))
        for d in range(1, NX)
    ]
    for c in x_copies:
        c.start()
    lax.fori_loop(49, PEERS, send_query, 0)

    for t in range(TILES):
        depth = (t + 1) * TILE
        row = lax.broadcasted_iota(jnp.int32, (depth, TILE), 0)
        column = lax.broadcasted_iota(jnp.int32, (depth, TILE), 1)
        mask = row <= column + t * TILE
        for h in range(HEADS):
            columns = slice(h * D_HEAD, (h + 1) * D_HEAD)
            out, lse = attend(
                k_ref[:depth, columns],
                v_ref[:depth, columns].T,
                q_ref[t * TILE : (t + 1) * TILE, columns],
                mask,
            )
            own_o[t * HEADS + h] = out
            own_l[t * HEADS + h] = lse
        if t == 1:
            w_hop_wait(2)
            w_hop(3)
        elif t == 2:
            w_hop_wait(3)
            w_hop(4)
    for h in range(HEADS):
        columns = slice(h * D_HEAD, (h + 1) * D_HEAD)
        vt[h] = pv_ref[:, columns].T
        kh[h] = pk_ref[:, columns]
    w_hop_wait(4)
    w_first(0)

    for d in range(1, NX):
        table_copy(9 + d, NZ * NY, place((x - d + NX) % NX, 0, 0), me).wait_recv()
    to_scalars = pltpu.make_async_copy(table, table_s, table_sem)
    to_scalars.start()
    to_scalars.wait()

    def o_copy(target, slot):
        return pltpu.make_async_remote_copy(
            src_ref=recv_q.at[target],
            dst_ref=recv_o.at[slot],
            send_sem=o_send_sem.at[target],
            recv_sem=o_recv_sem.at[slot],
            device_id={"ctx": target},
            device_id_type=pl.DeviceIdType.MESH,
        )

    def l_copy(target, slot):
        return pltpu.make_async_remote_copy(
            src_ref=send_l.at[target],
            dst_ref=recv_l.at[slot],
            send_sem=l_send_sem.at[target],
            recv_sem=l_recv_sem.at[slot],
            device_id={"ctx": target},
            device_id_type=pl.DeviceIdType.MESH,
        )

    def answer(source, query):
        head = table_s[source, 0, me] % HEADS
        return attend(kh[head], vt[head], query)

    out, lse = answer(me, items[wanted_ref[me]])
    recv_o[me] = out.astype(jnp.bfloat16)
    recv_l[me] = lse

    def serve(step, carry):
        source = moved(me, step, -sign)
        q_copy(me, source).wait_recv()
        out, lse = answer(source, recv_q[source])
        recv_q[source] = out.astype(jnp.bfloat16)
        send_l[source] = lse
        o_copy(source, me).start()
        l_copy(source, me).start()
        return carry

    lax.fori_loop(1, 9, serve, 0)
    w_forward(0)
    lax.fori_loop(9, 17, serve, 0)
    w_settle(0)
    w_first(1)
    def in_order(pair, carry):
        first = pair * 2
        bx, bz, by = coords(first)
        rows = pl.multiple_of(first * 8, 16)
        for p in range(2):
            if p == 0:
                one = (bx * NY + by) * NZ + bz
                two = one + NZ
            else:
                one = (by * NX + bx) * NZ + bz
                two = one + NX * NZ
            for g in range(2):
                wmat[g, pl.ds(rows, 16), p * W_HALF : (p + 1) * W_HALF] = jnp.concatenate(
                    [wbuf[p, one, g], wbuf[p, two, g]], axis=0
                )
        return carry

    lax.fori_loop(17, 56, serve, 0)
    w_forward(1)
    lax.fori_loop(56, 76, serve, 0)
    w_settle(1)
    lax.fori_loop(0, PEERS // 2, in_order, 0)
    lax.fori_loop(76, PEERS, serve, 0)


    def settle(step, carry):
        server = moved(me, step, sign)
        o_copy(me, server).wait_recv()
        l_copy(me, server).wait_recv()
        return carry

    lax.fori_loop(1, PEERS, settle, 0)

    def h_copy(t):
        return pltpu.make_async_remote_copy(
            src_ref=att.at[core, pl.ds(t * TILE, TILE)],
            dst_ref=att.at[core, pl.ds(t * TILE, TILE)],
            send_sem=h_send_sem.at[t],
            recv_sem=h_recv_sem.at[t],
            device_id={"head": 1 - core},
            device_id_type=pl.DeviceIdType.MESH,
        )

    for t in range(TILES):
        for h in range(HEADS):
            item = t * HEADS + h
            slots = [picked_ref[item * TOPK + j] for j in range(TOPK)]
            lses = [own_l[item]] + [recv_l[s] for s in slots]
            highest = functools.reduce(jnp.maximum, lses)
            factors = [jnp.exp2(v - highest) for v in lses]
            total = functools.reduce(jnp.add, factors)
            factors = [f * (1.0 / total) for f in factors]
            mixed = factors[0] * own_o[item]
            for f, s in zip(factors[1:], slots):
                mixed = mixed + f * recv_o[s].astype(jnp.float32)
            att[core, t * TILE : (t + 1) * TILE, h * D_HEAD : (h + 1) * D_HEAD] = (
                mixed.T.astype(jnp.bfloat16)
            )
        h_copy(t).start()

    def project_own(chunk, carry):
        columns = pl.ds(pl.multiple_of(chunk * CHUNK, CHUNK), CHUNK)
        acc[:, columns] = jnp.dot(
            att[core], wmat[core, :, columns], preferred_element_type=jnp.float32
        )
        return carry

    lax.fori_loop(0, 2 * W_HALF // CHUNK, project_own, 0)
    for t in range(TILES):
        pltpu.make_async_remote_copy(
            src_ref=att.at[1 - core, pl.ds(t * TILE, TILE)],
            dst_ref=att.at[1 - core, pl.ds(t * TILE, TILE)],
            send_sem=h_send_sem.at[t],
            recv_sem=h_recv_sem.at[t],
            device_id={"head": 1 - core},
            device_id_type=pl.DeviceIdType.MESH,
        ).wait_recv()

    def project_other(chunk, carry):
        columns = pl.ds(pl.multiple_of(chunk * CHUNK, CHUNK), CHUNK)
        other = jnp.dot(
            att[1 - core], wmat[1 - core, :, columns], preferred_element_type=jnp.float32
        )
        out_ref[:, columns] = (acc[:, columns] + other).astype(jnp.bfloat16)
        return carry

    lax.fori_loop(0, 2 * W_HALF // CHUNK, project_other, 0)
    for t in range(TILES):
        h_copy(t).wait_send()
    for p in range(2):
        s_copy(p).wait_send()

    def drain(step, carry):
        target = moved(me, step, sign)
        q_copy(target, me).wait_send()
        source = moved(me, step, -sign)
        o_copy(source, me).wait_send()
        l_copy(source, me).wait_send()
        return carry

    lax.fori_loop(1, PEERS, drain, 0)
    for c in y_copies + z_copies + x_copies + w_started:
        c.wait_send()


def layer(wanted, picked, queries, keys, values, prefix_keys, prefix_values, weight):
    vmem = pl.BlockSpec(memory_space=pltpu.VMEM)
    smem = pl.BlockSpec(memory_space=pltpu.SMEM)
    slots = (PEERS, TILE, D_HEAD)
    width = HEADS * D_HEAD
    sem = pltpu.SemaphoreType.DMA
    return pl.pallas_call(
        layer_kernel,
        out_shape=jax.ShapeDtypeStruct((BLOCK, 2 * W_HALF), jnp.bfloat16),
        in_specs=[smem, smem, vmem, vmem, vmem, vmem, vmem, vmem, vmem],
        out_specs=vmem,
        scratch_shapes=[
            pltpu.VMEM((ITEMS, TILE, D_HEAD), jnp.bfloat16),
            pltpu.VMEM(slots, jnp.bfloat16),
            pltpu.VMEM(slots, jnp.bfloat16),
            pltpu.VMEM(slots, jnp.bfloat16),
            pltpu.VMEM((PEERS, 1, TILE), jnp.float32),
            pltpu.VMEM((PEERS, 1, TILE), jnp.float32),
            pltpu.VMEM((HEADS, BLOCK, D_HEAD), jnp.bfloat16),
            pltpu.VMEM((HEADS, D_HEAD, BLOCK), jnp.bfloat16),
            pltpu.VMEM((2, PEERS, 2, 8, W_HALF), jnp.bfloat16),
            pltpu.VMEM((2, width, 2 * W_HALF), jnp.bfloat16),
            pltpu.VMEM((2, BLOCK, width), jnp.bfloat16),
            pltpu.VMEM((BLOCK, 2 * W_HALF), jnp.float32),
            pltpu.VMEM((ITEMS, D_HEAD, TILE), jnp.float32),
            pltpu.VMEM((ITEMS, 1, TILE), jnp.float32),
            pltpu.VMEM((PEERS, 1, PEERS), jnp.int32),
            pltpu.SMEM((PEERS, 1, PEERS), jnp.int32),
            sem,
            sem((PEERS,)),
            sem((PEERS,)),
            sem((PEERS,)),
            sem((PEERS,)),
            sem((PEERS,)),
            sem((PEERS,)),
            sem((13,)),
            sem((13,)),
            sem((TILES,)),
            sem((TILES,)),
            sem((2,)),
            sem((2,)),
            sem((2, 16)),
            sem((2, 16)),
        ],
        compiler_params=pltpu.CompilerParams(
            collective_id=0, has_side_effects=True, vmem_limit_bytes=60 * 1024 * 1024
        ),
    )(wanted, picked, wanted[None], queries, keys, values, prefix_keys, prefix_values, weight)


def shards(queries, keys, values, prefix_keys, prefix_values, selected, out_weight):
    picked = selected.reshape(ITEMS * TOPK)
    matches = picked[None, :] == jnp.arange(PEERS, dtype=jnp.int32)[:, None]
    item_ids = jnp.arange(ITEMS * TOPK, dtype=jnp.int32) // TOPK
    wanted = jnp.sum(jnp.where(matches, item_ids[None, :], 0), axis=1)
    return layer(
        wanted, picked, queries, keys, values, prefix_keys, prefix_values, out_weight[0]
    )


def solution(mesh):
    return jax.shard_map(
        shards,
        mesh=mesh,
        in_specs=(
            P("ctx", "head"),
            P("ctx", "head"),
            P("ctx", "head"),
            P("ctx", "head"),
            P("ctx", "head"),
            P("head", "ctx", None, None),
            P("head", "ctx", None),
        ),
        out_specs=P("ctx", "head"),
        check_vma=False,
    )
```

```python
import functools
import math

import jax
import jax.numpy as jnp
from jax import lax
from jax.experimental import pallas as pl
from jax.experimental.pallas import tpu as pltpu
from jax.sharding import PartitionSpec as P

D_HEAD = 128
TILE = 128
BLOCK = 512
TOPK = 3
TILES = 4
HEADS = 8
ITEMS = TILES * HEADS
W_HALF = 1024
CHUNK = 512
NX, NZ, NY = 4, 8, 4
PEERS = NX * NZ * NY
SCALE2 = D_HEAD**-0.5 * math.log2(math.e)


def coords(index):
    return index // (NZ * NY), (index // NY) % NZ, index % NY


def place(x, z, y):
    return (x * NZ + z) * NY + y


def offset_of(step):
    dz = (step * 3) % NZ
    dy = (step // NZ) % NY
    dx = (step // (NZ * NY)) % NX
    return dx, dz, dy


def moved(me, step, sign):
    x, z, y = coords(me)
    dx, dz, dy = offset_of(step)
    return place((x + sign * dx + NX) % NX, (z + sign * dz + NZ) % NZ, (y + sign * dy + NY) % NY)


def attend(key_block, value_block_t, query, mask=None):
    scores = lax.dot_general(
        key_block, query, (((1,), (1,)), ((), ())), preferred_element_type=jnp.float32
    )
    scores = scores * SCALE2
    if mask is not None:
        scores = jnp.where(mask, scores, -jnp.inf)
    top = jnp.max(scores, axis=0, keepdims=True)
    weights = jnp.exp2(scores - top)
    total = jnp.sum(weights, axis=0, keepdims=True)
    out = lax.dot_general(
        value_block_t,
        weights.astype(jnp.bfloat16),
        (((1,), (0,)), ((), ())),
        preferred_element_type=jnp.float32,
    )
    return out * (1.0 / total), top + jnp.log2(total)


def layer_kernel(
    wanted_ref,
    picked_ref,
    wanted_row_ref,
    q_ref,
    k_ref,
    v_ref,
    pk_ref,
    pv_ref,
    w_ref,
    out_ref,
    items,
    send_q,
    recv_q,
    recv_o,
    send_l,
    recv_l,
    kh,
    vt,
    wbuf,
    wmat,
    att,
    acc,
    own_o,
    own_l,
    table,
    table_s,
    table_sem,
    q_send_sem,
    q_recv_sem,
    o_send_sem,
    o_recv_sem,
    l_send_sem,
    l_recv_sem,
    t_send_sem,
    t_recv_sem,
    h_send_sem,
    h_recv_sem,
    s_send_sem,
    s_recv_sem,
    w_send_sem,
    w_recv_sem,
):
    me = lax.axis_index("ctx")
    core = lax.axis_index("head")
    x, z, y = coords(me)
    sign = 1 - 2 * core

    barrier = pltpu.get_barrier_semaphore()

    def greet(step, carry):
        pl.semaphore_signal(
            barrier,
            inc=1,
            device_id={"ctx": moved(me, step, 1)},
            device_id_type=pl.DeviceIdType.MESH,
        )
        return carry

    lax.fori_loop(1, PEERS, greet, 0)
    pl.semaphore_signal(
        barrier, inc=1, device_id={"head": 1 - core}, device_id_type=pl.DeviceIdType.MESH
    )

    for t in range(TILES):
        for h in range(HEADS):
            items[t * HEADS + h] = q_ref[
                t * TILE : (t + 1) * TILE, h * D_HEAD : (h + 1) * D_HEAD
            ]
    table[me] = wanted_row_ref[...]
    pl.semaphore_wait(barrier, PEERS)

    def table_copy(slot, rows, start, target):
        return pltpu.make_async_remote_copy(
            src_ref=table.at[pl.ds(start, rows)],
            dst_ref=table.at[pl.ds(start, rows)],
            send_sem=t_send_sem.at[slot],
            recv_sem=t_recv_sem.at[slot],
            device_id={"ctx": target},
            device_id_type=pl.DeviceIdType.MESH,
        )

    def w_major(p):
        return x if p == 0 else y

    def w_minor(p):
        return y if p == 0 else x

    def w_device(p, major, minor, depth):
        return place(major, depth, minor) if p == 0 else place(minor, depth, major)

    def w_pos(p):
        return (w_major(p) * NY + w_minor(p)) * NZ + z

    def w_copy(p, slot, start, blocks, target):
        return pltpu.make_async_remote_copy(
            src_ref=wbuf.at[p, pl.ds(start, blocks)],
            dst_ref=wbuf.at[p, pl.ds(start, blocks)],
            send_sem=w_send_sem.at[p, slot],
            recv_sem=w_recv_sem.at[p, slot],
            device_id={"ctx": target},
            device_id_type=pl.DeviceIdType.MESH,
        )

    def s_copy(p):
        columns = pl.multiple_of((1 - core) * 2 * W_HALF + p * W_HALF, W_HALF)
        return pltpu.make_async_remote_copy(
            src_ref=w_ref.at[:, pl.ds(columns, W_HALF)],
            dst_ref=wbuf.at[p, w_pos(p), core],
            send_sem=s_send_sem.at[p],
            recv_sem=s_recv_sem.at[p],
            device_id={"head": 1 - core},
            device_id_type=pl.DeviceIdType.MESH,
        )

    w_started = []

    def w_send(p, slot, start, blocks, target):
        c = w_copy(p, slot, start, blocks, target)
        c.start()
        w_started.append(c)

    def w_line(p, level, ahead):
        if level == 0:
            minor = (w_minor(p) + ahead + 4) % 4
            return (w_major(p) * 4 + minor) * NZ, w_device(p, w_major(p), minor, z)
        major = (w_major(p) + ahead + 4) % 4
        return major * 4 * NZ, w_device(p, major, w_minor(p), z)

    def w_first(level):
        blocks = (NZ, 4 * NZ)[level]
        for p in range(2):
            start = w_line(p, level, 0)[0]
            w_send(p, 8 + 4 * level, start, blocks, w_line(p, level, 1)[1])
            w_send(p, 9 + 4 * level, start, blocks, w_line(p, level, -1)[1])

    def w_forward(level):
        blocks = (NZ, 4 * NZ)[level]
        half = blocks // 2
        for p in range(2):
            behind, ahead = w_line(p, level, -1), w_line(p, level, 1)
            w_copy(p, 8 + 4 * level, behind[0], blocks, me).wait_recv()
            w_send(p, 10 + 4 * level, behind[0], half, ahead[1])
            w_copy(p, 9 + 4 * level, ahead[0], blocks, me).wait_recv()
            w_send(p, 11 + 4 * level, ahead[0] + half, half, behind[1])

    def w_settle(level):
        half = (NZ, 4 * NZ)[level] // 2
        for p in range(2):
            opposite = w_line(p, level, 2)[0]
            w_copy(p, 10 + 4 * level, opposite, half, me).wait_recv()
            w_copy(p, 11 + 4 * level, opposite + half, half, me).wait_recv()

    for p in range(2):
        s_copy(p).start()
        columns = pl.multiple_of(core * 2 * W_HALF + p * W_HALF, W_HALF)
        wbuf[p, w_pos(p), core] = w_ref[:, pl.ds(columns, W_HALF)]

    y_copies = [table_copy(d - 1, 1, me, place(x, z, (y + d) % NY)) for d in range(1, NY)]
    for c in y_copies:
        c.start()

    def w_ways(hop, p):
        return (0, 1) if hop < 4 else (p,)

    def w_block(p, ahead):
        return w_pos(p) - z + (z + ahead + NZ) % NZ

    def w_hop(hop):
        for p in range(2):
            for way in w_ways(hop, p):
                ahead = 1 - 2 * way
                w_send(
                    p,
                    2 * hop - 2 + way,
                    w_block(p, -ahead * (hop - 1)),
                    1,
                    place(x, (z + ahead + NZ) % NZ, y),
                )

    def w_hop_wait(hop):
        for p in range(2):
            for way in w_ways(hop, p):
                block = w_block(p, -(1 - 2 * way) * hop)
                w_copy(p, 2 * hop - 2 + way, block, 1, me).wait_recv()

    def q_copy(target, slot):
        return pltpu.make_async_remote_copy(
            src_ref=send_q.at[target],
            dst_ref=recv_q.at[slot],
            send_sem=q_send_sem.at[target],
            recv_sem=q_recv_sem.at[slot],
            device_id={"ctx": target},
            device_id_type=pl.DeviceIdType.MESH,
        )

    def send_query(step, carry):
        target = moved(me, step, sign)
        send_q[target] = items[wanted_ref[target]]
        q_copy(target, me).start()
        return carry

    lax.fori_loop(1, 17, send_query, 0)
    for p in range(2):
        pltpu.make_async_remote_copy(
            src_ref=w_ref.at[:, pl.ds(0, W_HALF)],
            dst_ref=wbuf.at[p, w_pos(p), 1 - core],
            send_sem=s_send_sem.at[p],
            recv_sem=s_recv_sem.at[p],
            device_id={"head": 1 - core},
            device_id_type=pl.DeviceIdType.MESH,
        ).wait_recv()
    w_hop(1)
    for d in range(1, NY):
        table_copy(d - 1, 1, place(x, z, (y - d + NY) % NY), me).wait_recv()
    z_copies = [
        table_copy(2 + d, NY, place(x, z, 0), place(x, (z + d) % NZ, y)) for d in range(1, NZ)
    ]
    for c in z_copies:
        c.start()
    lax.fori_loop(17, 49, send_query, 0)
    for d in range(1, NZ):
        table_copy(2 + d, NY, place(x, (z - d + NZ) % NZ, 0), me).wait_recv()
    x_copies = [
        table_copy(9 + d, NZ * NY, place(x, 0, 0), place((x + d) % NX, z, y))
        for d in range(1, NX)
    ]
    for c in x_copies:
        c.start()
    lax.fori_loop(49, PEERS, send_query, 0)

    for t in range(TILES):
        depth = (t + 1) * TILE
        row = lax.broadcasted_iota(jnp.int32, (depth, TILE), 0)
        column = lax.broadcasted_iota(jnp.int32, (depth, TILE), 1)
        mask = row <= column + t * TILE
        for h in range(HEADS):
            columns = slice(h * D_HEAD, (h + 1) * D_HEAD)
            out, lse = attend(
                k_ref[:depth, columns],
                v_ref[:depth, columns].T,
                q_ref[t * TILE : (t + 1) * TILE, columns],
                mask,
            )
            own_o[t * HEADS + h] = out
            own_l[t * HEADS + h] = lse
    for h in range(HEADS):
        columns = slice(h * D_HEAD, (h + 1) * D_HEAD)
        vt[h] = pv_ref[:, columns].T
        kh[h] = pk_ref[:, columns]
    w_hop_wait(1)
    w_hop(2)

    for d in range(1, NX):
        table_copy(9 + d, NZ * NY, place((x - d + NX) % NX, 0, 0), me).wait_recv()
    to_scalars = pltpu.make_async_copy(table, table_s, table_sem)
    to_scalars.start()
    to_scalars.wait()

    def o_copy(target, slot):
        return pltpu.make_async_remote_copy(
            src_ref=recv_q.at[target],
            dst_ref=recv_o.at[slot],
            send_sem=o_send_sem.at[target],
            recv_sem=o_recv_sem.at[slot],
            device_id={"ctx": target},
            device_id_type=pl.DeviceIdType.MESH,
        )

    def l_copy(target, slot):
        return pltpu.make_async_remote_copy(
            src_ref=send_l.at[target],
            dst_ref=recv_l.at[slot],
            send_sem=l_send_sem.at[target],
            recv_sem=l_recv_sem.at[slot],
            device_id={"ctx": target},
            device_id_type=pl.DeviceIdType.MESH,
        )

    def answer(source, query):
        head = table_s[source, 0, me] % HEADS
        return attend(kh[head], vt[head], query)

    out, lse = answer(me, items[wanted_ref[me]])
    recv_o[me] = out.astype(jnp.bfloat16)
    recv_l[me] = lse

    def serve(sources):
        for source in sources:
            q_copy(me, source).wait_recv()
        found = [answer(source, recv_q[source]) for source in sources]
        for source, (out, lse) in zip(sources, found):
            recv_q[source] = out.astype(jnp.bfloat16)
            send_l[source] = lse
            o_copy(source, me).start()
            l_copy(source, me).start()

    def serve_three(turn, carry):
        serve([moved(me, 2 + 3 * turn + j, -sign) for j in range(3)])
        return carry

    serve([moved(me, 1, -sign)])
    lax.fori_loop(0, 3, serve_three, 0)
    w_hop_wait(2)
    w_hop(3)
    lax.fori_loop(3, 6, serve_three, 0)
    w_hop_wait(3)
    w_hop(4)
    lax.fori_loop(6, 10, serve_three, 0)
    w_hop_wait(4)
    w_first(0)
    lax.fori_loop(10, 14, serve_three, 0)
    w_forward(0)
    lax.fori_loop(14, 18, serve_three, 0)
    w_settle(0)
    w_first(1)
    lax.fori_loop(18, 34, serve_three, 0)
    w_forward(1)
    lax.fori_loop(34, (PEERS - 2) // 3, serve_three, 0)

    w_settle(1)

    def in_order(pair, carry):
        first = pair * 2
        bx, bz, by = coords(first)
        rows = pl.multiple_of(first * 8, 16)
        for p in range(2):
            if p == 0:
                one = (bx * NY + by) * NZ + bz
                two = one + NZ
            else:
                one = (by * NX + bx) * NZ + bz
                two = one + NX * NZ
            for g in range(2):
                wmat[g, pl.ds(rows, 16), p * W_HALF : (p + 1) * W_HALF] = jnp.concatenate(
                    [wbuf[p, one, g], wbuf[p, two, g]], axis=0
                )
        return carry

    lax.fori_loop(0, PEERS // 2, in_order, 0)

    def settle(step, carry):
        server = moved(me, step, sign)
        o_copy(me, server).wait_recv()
        l_copy(me, server).wait_recv()
        return carry

    lax.fori_loop(1, PEERS, settle, 0)

    def h_copy(t):
        return pltpu.make_async_remote_copy(
            src_ref=att.at[core, pl.ds(t * TILE, TILE)],
            dst_ref=att.at[core, pl.ds(t * TILE, TILE)],
            send_sem=h_send_sem.at[t],
            recv_sem=h_recv_sem.at[t],
            device_id={"head": 1 - core},
            device_id_type=pl.DeviceIdType.MESH,
        )

    for t in range(TILES):
        for h in range(HEADS):
            item = t * HEADS + h
            slots = [picked_ref[item * TOPK + j] for j in range(TOPK)]
            lses = [own_l[item]] + [recv_l[s] for s in slots]
            highest = functools.reduce(jnp.maximum, lses)
            factors = [jnp.exp2(v - highest) for v in lses]
            total = functools.reduce(jnp.add, factors)
            factors = [f * (1.0 / total) for f in factors]
            mixed = factors[0] * own_o[item]
            for f, s in zip(factors[1:], slots):
                mixed = mixed + f * recv_o[s].astype(jnp.float32)
            att[core, t * TILE : (t + 1) * TILE, h * D_HEAD : (h + 1) * D_HEAD] = (
                mixed.T.astype(jnp.bfloat16)
            )
        h_copy(t).start()

    def project_own(chunk, carry):
        columns = pl.ds(pl.multiple_of(chunk * CHUNK, CHUNK), CHUNK)
        acc[:, columns] = jnp.dot(
            att[core], wmat[core, :, columns], preferred_element_type=jnp.float32
        )
        return carry

    lax.fori_loop(0, 2 * W_HALF // CHUNK, project_own, 0)
    for t in range(TILES):
        pltpu.make_async_remote_copy(
            src_ref=att.at[1 - core, pl.ds(t * TILE, TILE)],
            dst_ref=att.at[1 - core, pl.ds(t * TILE, TILE)],
            send_sem=h_send_sem.at[t],
            recv_sem=h_recv_sem.at[t],
            device_id={"head": 1 - core},
            device_id_type=pl.DeviceIdType.MESH,
        ).wait_recv()

    def project_other(chunk, carry):
        columns = pl.ds(pl.multiple_of(chunk * CHUNK, CHUNK), CHUNK)
        other = jnp.dot(
            att[1 - core], wmat[1 - core, :, columns], preferred_element_type=jnp.float32
        )
        out_ref[:, columns] = (acc[:, columns] + other).astype(jnp.bfloat16)
        return carry

    lax.fori_loop(0, 2 * W_HALF // CHUNK, project_other, 0)
    for t in range(TILES):
        h_copy(t).wait_send()
    for p in range(2):
        s_copy(p).wait_send()

    def drain(step, carry):
        target = moved(me, step, sign)
        q_copy(target, me).wait_send()
        source = moved(me, step, -sign)
        o_copy(source, me).wait_send()
        l_copy(source, me).wait_send()
        return carry

    lax.fori_loop(1, PEERS, drain, 0)
    for c in y_copies + z_copies + x_copies + w_started:
        c.wait_send()


def layer(wanted, picked, queries, keys, values, prefix_keys, prefix_values, weight):
    vmem = pl.BlockSpec(memory_space=pltpu.VMEM)
    smem = pl.BlockSpec(memory_space=pltpu.SMEM)
    slots = (PEERS, TILE, D_HEAD)
    width = HEADS * D_HEAD
    sem = pltpu.SemaphoreType.DMA
    return pl.pallas_call(
        layer_kernel,
        out_shape=jax.ShapeDtypeStruct((BLOCK, 2 * W_HALF), jnp.bfloat16),
        in_specs=[smem, smem, vmem, vmem, vmem, vmem, vmem, vmem, vmem],
        out_specs=vmem,
        scratch_shapes=[
            pltpu.VMEM((ITEMS, TILE, D_HEAD), jnp.bfloat16),
            pltpu.VMEM(slots, jnp.bfloat16),
            pltpu.VMEM(slots, jnp.bfloat16),
            pltpu.VMEM(slots, jnp.bfloat16),
            pltpu.VMEM((PEERS, 1, TILE), jnp.float32),
            pltpu.VMEM((PEERS, 1, TILE), jnp.float32),
            pltpu.VMEM((HEADS, BLOCK, D_HEAD), jnp.bfloat16),
            pltpu.VMEM((HEADS, D_HEAD, BLOCK), jnp.bfloat16),
            pltpu.VMEM((2, PEERS, 2, 8, W_HALF), jnp.bfloat16),
            pltpu.VMEM((2, width, 2 * W_HALF), jnp.bfloat16),
            pltpu.VMEM((2, BLOCK, width), jnp.bfloat16),
            pltpu.VMEM((BLOCK, 2 * W_HALF), jnp.float32),
            pltpu.VMEM((ITEMS, D_HEAD, TILE), jnp.float32),
            pltpu.VMEM((ITEMS, 1, TILE), jnp.float32),
            pltpu.VMEM((PEERS, 1, PEERS), jnp.int32),
            pltpu.SMEM((PEERS, 1, PEERS), jnp.int32),
            sem,
            sem((PEERS,)),
            sem((PEERS,)),
            sem((PEERS,)),
            sem((PEERS,)),
            sem((PEERS,)),
            sem((PEERS,)),
            sem((13,)),
            sem((13,)),
            sem((TILES,)),
            sem((TILES,)),
            sem((2,)),
            sem((2,)),
            sem((2, 16)),
            sem((2, 16)),
        ],
        compiler_params=pltpu.CompilerParams(
            collective_id=0, has_side_effects=True, vmem_limit_bytes=60 * 1024 * 1024
        ),
    )(wanted, picked, wanted[None], queries, keys, values, prefix_keys, prefix_values, weight)


def shards(queries, keys, values, prefix_keys, prefix_values, selected, out_weight):
    picked = selected.reshape(ITEMS * TOPK)
    matches = picked[None, :] == jnp.arange(PEERS, dtype=jnp.int32)[:, None]
    item_ids = jnp.arange(ITEMS * TOPK, dtype=jnp.int32) // TOPK
    wanted = jnp.sum(jnp.where(matches, item_ids[None, :], 0), axis=1)
    return layer(
        wanted, picked, queries, keys, values, prefix_keys, prefix_values, out_weight[0]
    )


def solution(mesh):
    return jax.shard_map(
        shards,
        mesh=mesh,
        in_specs=(
            P("ctx", "head"),
            P("ctx", "head"),
            P("ctx", "head"),
            P("ctx", "head"),
            P("ctx", "head"),
            P("head", "ctx", None, None),
            P("head", "ctx", None),
        ),
        out_specs=P("ctx", "head"),
        check_vma=False,
    )
```

```python
import functools
import math

import jax
import jax.numpy as jnp
from jax import lax
from jax.experimental import pallas as pl
from jax.experimental.pallas import tpu as pltpu
from jax.sharding import PartitionSpec as P

D_HEAD = 128
TILE = 128
BLOCK = 512
TOPK = 3
TILES = 4
HEADS = 8
ITEMS = TILES * HEADS
W_HALF = 1024
CHUNK = 512
NX, NZ, NY = 4, 8, 4
PEERS = NX * NZ * NY
SCALE2 = D_HEAD**-0.5 * math.log2(math.e)


def coords(index):
    return index // (NZ * NY), (index // NY) % NZ, index % NY


def place(x, z, y):
    return (x * NZ + z) * NY + y


def offset_of(step):
    dz = (step * 3) % NZ
    dy = (step // NZ) % NY
    dx = (step // (NZ * NY)) % NX
    return dx, dz, dy


def moved(me, step, sign):
    x, z, y = coords(me)
    dx, dz, dy = offset_of(step)
    return place((x + sign * dx + NX) % NX, (z + sign * dz + NZ) % NZ, (y + sign * dy + NY) % NY)


def attend(key_block, value_block_t, query, mask=None):
    scores = lax.dot_general(
        key_block, query, (((1,), (1,)), ((), ())), preferred_element_type=jnp.float32
    )
    scores = scores * SCALE2
    if mask is not None:
        scores = jnp.where(mask, scores, -jnp.inf)
    top = jnp.max(scores, axis=0, keepdims=True)
    weights = jnp.exp2(scores - top)
    total = jnp.sum(weights, axis=0, keepdims=True)
    out = lax.dot_general(
        value_block_t,
        weights.astype(jnp.bfloat16),
        (((1,), (0,)), ((), ())),
        preferred_element_type=jnp.float32,
    )
    return out * (1.0 / total), top + jnp.log2(total)


def layer_kernel(
    wanted_ref,
    picked_ref,
    wanted_row_ref,
    q_ref,
    k_ref,
    v_ref,
    pk_ref,
    pv_ref,
    w_ref,
    out_ref,
    items,
    send_q,
    recv_q,
    recv_o,
    send_l,
    recv_l,
    kh,
    vt,
    wbuf,
    wmat,
    att,
    acc,
    own_o,
    own_l,
    table,
    table_s,
    table_sem,
    q_send_sem,
    q_recv_sem,
    o_send_sem,
    o_recv_sem,
    l_send_sem,
    l_recv_sem,
    t_send_sem,
    t_recv_sem,
    h_send_sem,
    h_recv_sem,
    s_send_sem,
    s_recv_sem,
    w_send_sem,
    w_recv_sem,
):
    me = lax.axis_index("ctx")
    core = lax.axis_index("head")
    x, z, y = coords(me)
    sign = 1 - 2 * core

    barrier = pltpu.get_barrier_semaphore()

    def greet(step, carry):
        pl.semaphore_signal(
            barrier,
            inc=1,
            device_id={"ctx": moved(me, step, 1)},
            device_id_type=pl.DeviceIdType.MESH,
        )
        return carry

    lax.fori_loop(1, PEERS, greet, 0)
    pl.semaphore_signal(
        barrier, inc=1, device_id={"head": 1 - core}, device_id_type=pl.DeviceIdType.MESH
    )

    for t in range(TILES):
        for h in range(HEADS):
            items[t * HEADS + h] = q_ref[
                t * TILE : (t + 1) * TILE, h * D_HEAD : (h + 1) * D_HEAD
            ]
    table[me] = wanted_row_ref[...]
    pl.semaphore_wait(barrier, PEERS)

    def table_copy(slot, rows, start, target):
        return pltpu.make_async_remote_copy(
            src_ref=table.at[pl.ds(start, rows)],
            dst_ref=table.at[pl.ds(start, rows)],
            send_sem=t_send_sem.at[slot],
            recv_sem=t_recv_sem.at[slot],
            device_id={"ctx": target},
            device_id_type=pl.DeviceIdType.MESH,
        )

    def w_major(p):
        return x if p == 0 else y

    def w_minor(p):
        return y if p == 0 else x

    def w_device(p, major, minor, depth):
        return place(major, depth, minor) if p == 0 else place(minor, depth, major)

    def w_pos(p):
        return (w_major(p) * NY + w_minor(p)) * NZ + z

    def w_copy(p, slot, start, blocks, target):
        return pltpu.make_async_remote_copy(
            src_ref=wbuf.at[p, pl.ds(start, blocks)],
            dst_ref=wbuf.at[p, pl.ds(start, blocks)],
            send_sem=w_send_sem.at[p, slot],
            recv_sem=w_recv_sem.at[p, slot],
            device_id={"ctx": target},
            device_id_type=pl.DeviceIdType.MESH,
        )

    def s_copy(p):
        columns = pl.multiple_of((1 - core) * 2 * W_HALF + p * W_HALF, W_HALF)
        return pltpu.make_async_remote_copy(
            src_ref=w_ref.at[:, pl.ds(columns, W_HALF)],
            dst_ref=wbuf.at[p, w_pos(p), core],
            send_sem=s_send_sem.at[p],
            recv_sem=s_recv_sem.at[p],
            device_id={"head": 1 - core},
            device_id_type=pl.DeviceIdType.MESH,
        )

    w_started = []

    def w_send(p, slot, start, blocks, target):
        c = w_copy(p, slot, start, blocks, target)
        c.start()
        w_started.append(c)

    def w_line(p, level, ahead):
        if level == 0:
            minor = (w_minor(p) + ahead + 4) % 4
            return (w_major(p) * 4 + minor) * NZ, w_device(p, w_major(p), minor, z)
        major = (w_major(p) + ahead + 4) % 4
        return major * 4 * NZ, w_device(p, major, w_minor(p), z)

    def w_first(level):
        blocks = (NZ, 4 * NZ)[level]
        for p in range(2):
            start = w_line(p, level, 0)[0]
            w_send(p, 7 + 4 * level, start, blocks, w_line(p, level, 1)[1])
            w_send(p, 8 + 4 * level, start, blocks, w_line(p, level, -1)[1])

    def w_forward(level):
        blocks = (NZ, 4 * NZ)[level]
        half = blocks // 2
        for p in range(2):
            behind, ahead = w_line(p, level, -1), w_line(p, level, 1)
            w_copy(p, 7 + 4 * level, behind[0], blocks, me).wait_recv()
            w_send(p, 9 + 4 * level, behind[0], half, ahead[1])
            w_copy(p, 8 + 4 * level, ahead[0], blocks, me).wait_recv()
            w_send(p, 10 + 4 * level, ahead[0] + half, half, behind[1])

    def w_settle(level):
        half = (NZ, 4 * NZ)[level] // 2
        for p in range(2):
            opposite = w_line(p, level, 2)[0]
            w_copy(p, 9 + 4 * level, opposite, half, me).wait_recv()
            w_copy(p, 10 + 4 * level, opposite + half, half, me).wait_recv()

    for p in range(2):
        s_copy(p).start()
        columns = pl.multiple_of(core * 2 * W_HALF + p * W_HALF, W_HALF)
        wbuf[p, w_pos(p), core] = w_ref[:, pl.ds(columns, W_HALF)]

    y_copies = [table_copy(d - 1, 1, me, place(x, z, (y + d) % NY)) for d in range(1, NY)]
    for c in y_copies:
        c.start()

    for p in range(2):
        pltpu.make_async_remote_copy(
            src_ref=w_ref.at[:, pl.ds(0, W_HALF)],
            dst_ref=wbuf.at[p, w_pos(p), 1 - core],
            send_sem=s_send_sem.at[p],
            recv_sem=s_recv_sem.at[p],
            device_id={"head": 1 - core},
            device_id_type=pl.DeviceIdType.MESH,
        ).wait_recv()
        for d in range(1, NZ):
            w_send(
                p,
                d - 1,
                w_pos(p),
                1,
                w_device(p, w_major(p), w_minor(p), (z + d) % NZ),
            )

    def q_copy(target, slot):
        return pltpu.make_async_remote_copy(
            src_ref=send_q.at[target],
            dst_ref=recv_q.at[slot],
            send_sem=q_send_sem.at[target],
            recv_sem=q_recv_sem.at[slot],
            device_id={"ctx": target},
            device_id_type=pl.DeviceIdType.MESH,
        )

    def send_query(step, carry):
        target = moved(me, step, sign)
        send_q[target] = items[wanted_ref[target]]
        q_copy(target, me).start()
        return carry

    lax.fori_loop(1, 17, send_query, 0)
    for p in range(2):
        base = w_pos(p) - z
        for d in range(1, NZ):
            w_copy(p, d - 1, base + (z - d + NZ) % NZ, 1, me).wait_recv()
    w_first(0)
    for d in range(1, NY):
        table_copy(d - 1, 1, place(x, z, (y - d + NY) % NY), me).wait_recv()
    z_copies = [
        table_copy(2 + d, NY, place(x, z, 0), place(x, (z + d) % NZ, y)) for d in range(1, NZ)
    ]
    for c in z_copies:
        c.start()
    lax.fori_loop(17, 33, send_query, 0)
    w_forward(0)
    for d in range(1, NZ):
        table_copy(2 + d, NY, place(x, (z - d + NZ) % NZ, 0), me).wait_recv()
    x_copies = [
        table_copy(9 + d, NZ * NY, place(x, 0, 0), place((x + d) % NX, z, y))
        for d in range(1, NX)
    ]
    for c in x_copies:
        c.start()
    lax.fori_loop(33, 41, send_query, 0)
    w_settle(0)
    w_first(1)
    lax.fori_loop(41, PEERS, send_query, 0)

    for t in range(TILES):
        depth = (t + 1) * TILE
        row = lax.broadcasted_iota(jnp.int32, (depth, TILE), 0)
        column = lax.broadcasted_iota(jnp.int32, (depth, TILE), 1)
        mask = row <= column + t * TILE
        for h in range(HEADS):
            columns = slice(h * D_HEAD, (h + 1) * D_HEAD)
            out, lse = attend(
                k_ref[:depth, columns],
                v_ref[:depth, columns].T,
                q_ref[t * TILE : (t + 1) * TILE, columns],
                mask,
            )
            own_o[t * HEADS + h] = out
            own_l[t * HEADS + h] = lse
    for h in range(HEADS):
        columns = slice(h * D_HEAD, (h + 1) * D_HEAD)
        vt[h] = pv_ref[:, columns].T
        kh[h] = pk_ref[:, columns]

    for d in range(1, NX):
        table_copy(9 + d, NZ * NY, place((x - d + NX) % NX, 0, 0), me).wait_recv()
    to_scalars = pltpu.make_async_copy(table, table_s, table_sem)
    to_scalars.start()
    to_scalars.wait()

    def o_copy(target, slot):
        return pltpu.make_async_remote_copy(
            src_ref=recv_q.at[target],
            dst_ref=recv_o.at[slot],
            send_sem=o_send_sem.at[target],
            recv_sem=o_recv_sem.at[slot],
            device_id={"ctx": target},
            device_id_type=pl.DeviceIdType.MESH,
        )

    def l_copy(target, slot):
        return pltpu.make_async_remote_copy(
            src_ref=send_l.at[target],
            dst_ref=recv_l.at[slot],
            send_sem=l_send_sem.at[target],
            recv_sem=l_recv_sem.at[slot],
            device_id={"ctx": target},
            device_id_type=pl.DeviceIdType.MESH,
        )

    def answer(source, query):
        head = table_s[source, 0, me] % HEADS
        return attend(kh[head], vt[head], query)

    out, lse = answer(me, items[wanted_ref[me]])
    recv_o[me] = out.astype(jnp.bfloat16)
    recv_l[me] = lse

    def serve(step, carry):
        source = moved(me, step, -sign)
        q_copy(me, source).wait_recv()
        out, lse = answer(source, recv_q[source])
        recv_q[source] = out.astype(jnp.bfloat16)
        send_l[source] = lse
        o_copy(source, me).start()
        l_copy(source, me).start()
        return carry

    lax.fori_loop(1, 56, serve, 0)
    w_forward(1)
    lax.fori_loop(56, PEERS, serve, 0)

    w_settle(1)

    def in_order(pair, carry):
        first = pair * 2
        bx, bz, by = coords(first)
        rows = pl.multiple_of(first * 8, 16)
        for p in range(2):
            if p == 0:
                one = (bx * NY + by) * NZ + bz
                two = one + NZ
            else:
                one = (by * NX + bx) * NZ + bz
                two = one + NX * NZ
            for g in range(2):
                wmat[g, pl.ds(rows, 16), p * W_HALF : (p + 1) * W_HALF] = jnp.concatenate(
                    [wbuf[p, one, g], wbuf[p, two, g]], axis=0
                )
        return carry

    lax.fori_loop(0, PEERS // 2, in_order, 0)

    def settle(step, carry):
        server = moved(me, step, sign)
        o_copy(me, server).wait_recv()
        l_copy(me, server).wait_recv()
        return carry

    lax.fori_loop(1, PEERS, settle, 0)

    def h_copy(t):
        return pltpu.make_async_remote_copy(
            src_ref=att.at[core, pl.ds(t * TILE, TILE)],
            dst_ref=att.at[core, pl.ds(t * TILE, TILE)],
            send_sem=h_send_sem.at[t],
            recv_sem=h_recv_sem.at[t],
            device_id={"head": 1 - core},
            device_id_type=pl.DeviceIdType.MESH,
        )

    for t in range(TILES):
        for h in range(HEADS):
            item = t * HEADS + h
            slots = [picked_ref[item * TOPK + j] for j in range(TOPK)]
            lses = [own_l[item]] + [recv_l[s] for s in slots]
            highest = functools.reduce(jnp.maximum, lses)
            factors = [jnp.exp2(v - highest) for v in lses]
            total = functools.reduce(jnp.add, factors)
            mixed = factors[0] * own_o[item]
            for f, s in zip(factors[1:], slots):
                mixed = mixed + f * recv_o[s].astype(jnp.float32)
            mixed = mixed / total
            att[core, t * TILE : (t + 1) * TILE, h * D_HEAD : (h + 1) * D_HEAD] = (
                mixed.T.astype(jnp.bfloat16)
            )
        h_copy(t).start()

    def project_own(chunk, carry):
        columns = pl.ds(pl.multiple_of(chunk * CHUNK, CHUNK), CHUNK)
        acc[:, columns] = jnp.dot(
            att[core], wmat[core, :, columns], preferred_element_type=jnp.float32
        )
        return carry

    lax.fori_loop(0, 2 * W_HALF // CHUNK, project_own, 0)
    for t in range(TILES):
        pltpu.make_async_remote_copy(
            src_ref=att.at[1 - core, pl.ds(t * TILE, TILE)],
            dst_ref=att.at[1 - core, pl.ds(t * TILE, TILE)],
            send_sem=h_send_sem.at[t],
            recv_sem=h_recv_sem.at[t],
            device_id={"head": 1 - core},
            device_id_type=pl.DeviceIdType.MESH,
        ).wait_recv()

    def project_other(chunk, carry):
        columns = pl.ds(pl.multiple_of(chunk * CHUNK, CHUNK), CHUNK)
        other = jnp.dot(
            att[1 - core], wmat[1 - core, :, columns], preferred_element_type=jnp.float32
        )
        out_ref[:, columns] = (acc[:, columns] + other).astype(jnp.bfloat16)
        return carry

    lax.fori_loop(0, 2 * W_HALF // CHUNK, project_other, 0)
    for t in range(TILES):
        h_copy(t).wait_send()
    for p in range(2):
        s_copy(p).wait_send()

    def drain(step, carry):
        target = moved(me, step, sign)
        q_copy(target, me).wait_send()
        source = moved(me, step, -sign)
        o_copy(source, me).wait_send()
        l_copy(source, me).wait_send()
        return carry

    lax.fori_loop(1, PEERS, drain, 0)
    for c in y_copies + z_copies + x_copies + w_started:
        c.wait_send()


def layer(wanted, picked, queries, keys, values, prefix_keys, prefix_values, weight):
    vmem = pl.BlockSpec(memory_space=pltpu.VMEM)
    smem = pl.BlockSpec(memory_space=pltpu.SMEM)
    slots = (PEERS, TILE, D_HEAD)
    width = HEADS * D_HEAD
    sem = pltpu.SemaphoreType.DMA
    return pl.pallas_call(
        layer_kernel,
        out_shape=jax.ShapeDtypeStruct((BLOCK, 2 * W_HALF), jnp.bfloat16),
        in_specs=[smem, smem, vmem, vmem, vmem, vmem, vmem, vmem, vmem],
        out_specs=vmem,
        scratch_shapes=[
            pltpu.VMEM((ITEMS, TILE, D_HEAD), jnp.bfloat16),
            pltpu.VMEM(slots, jnp.bfloat16),
            pltpu.VMEM(slots, jnp.bfloat16),
            pltpu.VMEM(slots, jnp.bfloat16),
            pltpu.VMEM((PEERS, 1, TILE), jnp.float32),
            pltpu.VMEM((PEERS, 1, TILE), jnp.float32),
            pltpu.VMEM((HEADS, BLOCK, D_HEAD), jnp.bfloat16),
            pltpu.VMEM((HEADS, D_HEAD, BLOCK), jnp.bfloat16),
            pltpu.VMEM((2, PEERS, 2, 8, W_HALF), jnp.bfloat16),
            pltpu.VMEM((2, width, 2 * W_HALF), jnp.bfloat16),
            pltpu.VMEM((2, BLOCK, width), jnp.bfloat16),
            pltpu.VMEM((BLOCK, 2 * W_HALF), jnp.float32),
            pltpu.VMEM((ITEMS, D_HEAD, TILE), jnp.float32),
            pltpu.VMEM((ITEMS, 1, TILE), jnp.float32),
            pltpu.VMEM((PEERS, 1, PEERS), jnp.int32),
            pltpu.SMEM((PEERS, 1, PEERS), jnp.int32),
            sem,
            sem((PEERS,)),
            sem((PEERS,)),
            sem((PEERS,)),
            sem((PEERS,)),
            sem((PEERS,)),
            sem((PEERS,)),
            sem((13,)),
            sem((13,)),
            sem((TILES,)),
            sem((TILES,)),
            sem((2,)),
            sem((2,)),
            sem((2, 15)),
            sem((2, 15)),
        ],
        compiler_params=pltpu.CompilerParams(
            collective_id=0, has_side_effects=True, vmem_limit_bytes=60 * 1024 * 1024
        ),
    )(wanted, picked, wanted[None], queries, keys, values, prefix_keys, prefix_values, weight)


def shards(queries, keys, values, prefix_keys, prefix_values, selected, out_weight):
    picked = selected.reshape(ITEMS * TOPK)
    matches = picked[None, :] == jnp.arange(PEERS, dtype=jnp.int32)[:, None]
    item_ids = jnp.arange(ITEMS * TOPK, dtype=jnp.int32) // TOPK
    wanted = jnp.sum(jnp.where(matches, item_ids[None, :], 0), axis=1)
    return layer(
        wanted, picked, queries, keys, values, prefix_keys, prefix_values, out_weight[0]
    )


def solution(mesh):
    return jax.shard_map(
        shards,
        mesh=mesh,
        in_specs=(
            P("ctx", "head"),
            P("ctx", "head"),
            P("ctx", "head"),
            P("ctx", "head"),
            P("ctx", "head"),
            P("head", "ctx", None, None),
            P("head", "ctx", None),
        ),
        out_specs=P("ctx", "head"),
        check_vma=False,
    )
```
